128 devices in a mesh: fsdp: 32 (over y, z, core), tensor: 4 (over x).
Axes of the slice: x: 4, y: 4, z: 4, core: 2. Of those that a mesh axis runs over, the one named last changes fastest.
Arguments:
- item_hidden: bfloat16 [65536, 4096], P('fsdp', 'tensor'), may hold values from -700 to 700
- item_gain: float32 [4096], P('tensor'), may hold values from 0.5 to 2
- occ_owner: int32 [8192, 1], P('fsdp'), may hold values from 0 to 31; in each aligned block of 256 rows (0 to 255, 256 to 511, ...) at most 16 rows name the same one
- occ_item: int32 [8192], P('fsdp'), may hold values from 0 to 255
- hist_len: int32 [32], P('fsdp'), may hold values from 128 to 256, as said below
- user_gain: float32 [4096], replicated, may hold values from 0.5 to 2
- wqkv: bfloat16 [3, 4096, 4096], P(None, 'fsdp', 'tensor'), may hold values from -2 to 2
- grad_out: bfloat16 [8192, 4096], P('fsdp', 'tensor'), may hold values from -6 to 6
Outputs:
- item_embed: bfloat16 [8192, 4096], P('fsdp', 'tensor')
- attn_out: bfloat16 [8192, 4096], P('fsdp', 'tensor')
- item_grads: float32 [8192, 4096], P('fsdp', 'tensor')
The draws below stay inside these ranges and needn't reach their ends.
Inputs may be any that keep to these rules, and one draw needn't show every extreme that they name: `occ_owner`: among the 256 positions of one history, at most 16 name items of the same owner, a bound that some block reaches. `hist_len`: a multiple of 128; positions at or beyond it are padding; some history has the full 256.
All inputs are finite; a program needn't handle non-finite values.
Results may differ from the reference program's by a relative error of at most 0.022.
The reference program's roundings to bfloat16 on the way count: a program that leaves them out, or rounds other values in their place, can miss the bound.
Values may be sent and summed in bfloat16 or wider, within the bound.
A program may use at most 128 MiB of HBM per device.

```python
import functools
import math
import jax
import jax.numpy as jnp
import numpy as np
from jax import lax

D = 4096
HEADS = 32
HEAD_DIM = 128
ITEMS_DEV = 256
ITEM_LEN = 8
HLEN = 256
LBLK = 128
CAP = 16
ITEMS = 8192
HISTS = 32
HIST_POS = 8192
N_FSDP = 32
N_TENSOR = 4


def shared_profile(key):
    k_cols = jax.random.fold_in(jax.random.fold_in(key, 5), 0)
    columns = 10.0 ** (0.5 * jnp.arange(D, dtype=jnp.float32) / D + 0.5 * jax.random.uniform(k_cols, (D,), jnp.float32))
    return columns


def draw_item_hidden(key, part):
    columns = shared_profile(key)
    key = jax.random.fold_in(key, 11)
    k_noise, k_rows = jax.random.split(key, 2)
    total_rows = ITEMS * ITEM_LEN
    random_part = jnp.clip(jax.random.normal(k_noise, (total_rows, D), jnp.float32), -4.0, 4.0)
    rows_scale = 10.0 ** jax.random.uniform(k_rows, (total_rows, 1), jnp.float32)
    return (random_part * rows_scale * columns).astype(jnp.bfloat16)


def draw_wqkv(key, part):
    key = jax.random.fold_in(key, 23)
    k_base = jax.random.fold_in(key, 0)
    weights = jnp.clip(jax.random.normal(k_base, (3, D, D), jnp.float32), -4.0, 4.0) * D ** (-0.5)
    return weights.astype(jnp.bfloat16)


def draw_hist_len(key, part):
    key = jax.random.fold_in(key, 37)
    k_blocks, k_pick = jax.random.split(key)
    most_blocks = HLEN // LBLK
    blocks = jax.random.randint(k_blocks, (HISTS,), 1, most_blocks + 1)
    chosen = jax.random.randint(k_pick, (), 0, HISTS)
    blocks = jnp.where(jnp.arange(HISTS) == chosen, most_blocks, blocks)
    return (blocks * LBLK).astype(jnp.int32)


def touch_ends(array, stream_key, least, largest):
    longest = array.shape.index(max(array.shape))
    spots = []
    for shift in (0, 1):
        where = [jax.random.randint(jax.random.fold_in(stream_key, axis), (), 0, length) for axis, length in enumerate(array.shape)]
        where[longest] = (where[longest] + shift) % array.shape[longest]
        spots.append(tuple(where))
    return array.at[spots[0]].set(least).at[spots[1]].set(largest)


def steps_of(rng, shape, cuts, low, high):
    def one(dim, parts):
        steps = jax.random.uniform(jax.random.fold_in(jax.random.fold_in(rng, 6), dim), (parts,), jnp.float32, low / len(cuts), high / len(cuts))
        return jnp.repeat(jnp.exp(steps), shape[dim] // parts).reshape((-1,) + (1,) * (len(shape) - dim - 1))

    loudness = one(*cuts[0])
    for cut in cuts[1:]:
        loudness = loudness * one(*cut)
    return loudness


def shared_out(own_key, own, number, rows, number_of, top, limit, lean):
    ranking = jax.random.permutation(own_key, number_of)
    heavy_load, usual = shares(number_of, rows * top, limit, lean, True), shares(number_of, rows * top, limit, lean, False)
    places = jnp.arange(number_of)

    def named(lengths, rotation):
        used = int((lengths > 0).sum())
        fixed = max(1, used // 4)
        moved = fixed + (places - fixed + rotation * (used - fixed)) % max(1, number_of - fixed)
        return jnp.zeros((number_of,), jnp.int32).at[ranking[jnp.where(places < fixed, places, moved)]].set(jnp.asarray(lengths, jnp.int32))

    lengths = jnp.where(number % 4 == 0, named(heavy_load, number // 4), named(usual, number - number // 4 - 1))
    mixed = jax.random.permutation(jax.random.fold_in(own, 3), number_of)
    giver, sink = mixed[0:number_of // 2 * 2:2], mixed[1:number_of // 2 * 2:2]
    slack = jnp.minimum(lengths[giver] - 1, limit - lengths[sink]) // 2
    slack = jnp.where((giver == ranking[0]) | (sink == ranking[0]) | (lengths[sink] == 0), 0, jnp.maximum(slack, 0))
    moved = jax.random.randint(jax.random.fold_in(own, 4), (number_of // 2,), 0, 1 << 20) % (slack + 1)
    lengths = lengths.at[giver].add(-moved).at[sink].add(moved)
    labels = jnp.searchsorted(jnp.cumsum(lengths), jnp.arange(rows * top), side="right").astype(jnp.int32)
    grid = labels.reshape(top, rows).T
    grid = grid[jax.random.permutation(jax.random.fold_in(own, 1), rows)]
    rotation = jax.random.randint(jax.random.fold_in(own, 2), (rows, 1), 0, top)
    return jnp.take_along_axis(grid, (jnp.arange(top)[None, :] + rotation) % top, axis=1)


def shares(amount, total, most, slope, full):
    weights = [(1 << 20) // math.isqrt(grade ** slope) + 1 for grade in range(1, amount + 1)]
    largest = most if full else min(most, max(-(-total // amount), total * weights[0] // sum(weights)))
    least = 1 if total - largest >= amount - 1 else 0
    holding, rest = [largest] + [least] * (amount - 1), total - largest - least * (amount - 1)
    while rest > 0:
        free = [i for i in range(1, amount) if holding[i] < largest] or [i for i in range(1, amount) if holding[i] < most]
        whole, remaining = sum([weights[i] for i in free]), rest
        for i in free:
            more = min(most - holding[i], max(1, remaining * weights[i] // whole), rest)
            holding[i] = holding[i] + more
            rest = rest - more
    return np.array(holding)


def normal_values(rng, shape, scale, most, cuts=(), kind=jnp.bfloat16):
    entries = scale * jax.random.normal(rng, shape, jnp.float32)
    if cuts:
        entries = entries * steps_of(rng, shape, cuts, -0.22, 0.18)
    return jnp.clip(entries, -most, most).astype(kind)


def setup_inputs(seed: int = 0) -> dict:
    arg_keys = jax.random.split(jax.random.key(seed), 9)
    item_hidden = draw_item_hidden(jax.random.fold_in(arg_keys[8], 71), 0)
    item_gain = jnp.clip(jnp.exp(math.log(2.0) - 1.3862944 * jax.random.uniform(arg_keys[1], (D,), jnp.float32) ** steps_of(arg_keys[1], (D,), ((0, 4),), -0.2, 0.2)), 0.5, 2.0)
    occ_owner_keys = jax.random.split(jax.random.fold_in(arg_keys[2], 1), HIST_POS // HLEN)
    occ_owner_turns = jax.random.permutation(jax.random.fold_in(arg_keys[2], 3), HIST_POS // HLEN)
    occ_owner = jax.vmap(lambda own, number: shared_out(jax.random.fold_in(arg_keys[2], 2), own, number, HLEN, N_FSDP, 1, CAP, 2))(occ_owner_keys, occ_owner_turns).reshape((HIST_POS, 1))
    occ_item = touch_ends(jax.random.randint(arg_keys[3], (HIST_POS,), 0, ITEMS_DEV), jax.random.fold_in(arg_keys[3], 1), 0, ITEMS_DEV - 1).astype(jnp.int32)
    hist_len = draw_hist_len(jax.random.fold_in(arg_keys[8], 71), 0)
    user_gain = jnp.clip(jnp.exp(jax.random.uniform(arg_keys[5], (D,), jnp.float32, math.log(0.5), math.log(2.0))), 0.5, 2.0)
    wqkv = draw_wqkv(jax.random.fold_in(arg_keys[8], 71), 0)
    grad_out = normal_values(arg_keys[7], (HIST_POS, D), 1.0, 6.0, ((0, 32), (1, 4)))
    return dict(item_hidden=item_hidden, item_gain=item_gain, occ_owner=occ_owner, occ_item=occ_item, hist_len=hist_len, user_gain=user_gain, wqkv=wqkv, grad_out=grad_out)


EPSILON = 1e-05

def attend(queries, key_rows, value_rows, upstream_in, length):
    extent = queries.shape[0]
    factor = 1.0 / math.sqrt(queries.shape[2])
    places = jnp.arange(extent, dtype=jnp.int32)
    allowed = (places[None, :] <= places[:, None]) & (places[None, :] < length)
    active = places < length
    q_f = queries.astype(jnp.float32)
    k_f = key_rows.astype(jnp.float32)
    v_f = value_rows.astype(jnp.float32)
    scores = jnp.einsum('qhe,khe->hqk', q_f, k_f) * factor
    scores = jnp.where(allowed[None], scores, jnp.float32(-1e+30))
    row_max = lax.optimization_barrier(jnp.max(scores, axis=2, keepdims=True))
    raised = jnp.where(allowed[None], jnp.exp(scores - row_max), jnp.float32(0.0))
    weights_f = raised / lax.optimization_barrier(jnp.sum(raised, axis=2, keepdims=True))
    weights_b = weights_f.astype(jnp.bfloat16).astype(jnp.float32)
    attended = jnp.einsum('hqk,khe->qhe', weights_b, v_f)
    attended = jnp.where(active[:, None, None], attended, jnp.float32(0.0)).astype(jnp.bfloat16)
    upstream = jnp.where(active[:, None, None], upstream_in.astype(jnp.float32), jnp.float32(0.0))
    grad_v = jnp.einsum('hqk,qhe->khe', weights_b, upstream).astype(jnp.bfloat16)
    grad_p = jnp.einsum('qhe,khe->hqk', upstream, v_f)
    row_dot = lax.optimization_barrier(jnp.sum(weights_f * grad_p, axis=2, keepdims=True))
    grad_s = (weights_f * (grad_p - row_dot) * factor).astype(jnp.bfloat16).astype(jnp.float32)
    grad_q = jnp.einsum('hqk,khe->qhe', grad_s, k_f).astype(jnp.bfloat16)
    grad_k = jnp.einsum('hqk,qhe->khe', grad_s, q_f).astype(jnp.bfloat16)
    return (attended, grad_q, grad_k, grad_v)

def pool_items(item_gain, item_block):
    values = item_block.astype(jnp.float32)
    inverse = lax.rsqrt(lax.optimization_barrier(jnp.sum(values * values, axis=1, keepdims=True)) / D + EPSILON)
    normed = values * inverse * item_gain
    return lax.optimization_barrier(jnp.mean(normed.reshape(ITEMS_DEV, ITEM_LEN, D), axis=1)).astype(jnp.bfloat16)

def history_pass(user_gain, w_full, packed):
    history, upstream, length = packed
    inputs = history.astype(jnp.float32)
    inverse = lax.rsqrt(lax.optimization_barrier(jnp.sum(inputs * inputs, axis=1, keepdims=True)) / D + EPSILON)
    normed = (inputs * inverse * user_gain).astype(jnp.bfloat16)
    projected = jnp.einsum('td,cde->cte', normed.astype(jnp.float32), w_full).astype(jnp.bfloat16)
    shaped = projected.reshape(3, HLEN, HEADS, HEAD_DIM)
    attended, grad_q, grad_k, grad_v = attend(shaped[0], shaped[1], shaped[2], upstream.reshape(HLEN, HEADS, HEAD_DIM), length)
    grads = jnp.stack([grad_q, grad_k, grad_v]).astype(jnp.float32).reshape(3, HLEN, N_TENSOR, D // N_TENSOR)
    partials = jnp.einsum('ctge,cdge->gtd', grads, w_full.reshape(3, D, N_TENSOR, D // N_TENSOR))
    rounded = lax.optimization_barrier(partials.astype(jnp.bfloat16)).astype(jnp.float32)
    grad_normed = lax.optimization_barrier(jnp.sum(rounded, axis=0))
    scaled = grad_normed * user_gain
    row_stat = lax.optimization_barrier(jnp.sum(inputs * scaled, axis=1, keepdims=True)) / D
    grad_in = (inverse * scaled - inputs * inverse ** 3 * row_stat).astype(jnp.bfloat16)
    return (attended.reshape(HLEN, D), grad_in)

def reference(item_hidden, item_gain, occ_owner, occ_item, hist_len, user_gain, wqkv, grad_out):
    item_embed = lax.map(functools.partial(pool_items, item_gain), item_hidden.reshape(N_FSDP, ITEMS_DEV * ITEM_LEN, D)).reshape(ITEMS, D)
    item_ids = (occ_owner[:, 0] * ITEMS_DEV + occ_item).astype(jnp.int32)
    gathered = item_embed[item_ids]
    w_full = wqkv.astype(jnp.float32)
    attended, grad_in = lax.map(functools.partial(history_pass, user_gain, w_full), (gathered.reshape(HISTS, HLEN, D), grad_out.reshape(HISTS, HLEN, D), hist_len))
    item_grads = jax.ops.segment_sum(grad_in.reshape(HIST_POS, D).astype(jnp.float32), item_ids, num_segments=ITEMS)
    return (item_embed, attended.reshape(HIST_POS, D), item_grads)
```

```python
import functools
import math

import jax
import jax.numpy as jnp
from jax import lax
from jax.experimental import pallas as pl
from jax.experimental.pallas import tpu as pltpu
from jax.sharding import PartitionSpec as P

D = 4096
HEAD_DIM = 128
ITEM_LEN = 8
EPSILON = 1e-05
NF = 32
NX = 4
ROWS = 256
CAP = 16
SLOTS = NF * CAP
WIDTH = D // NX
HALF = WIDTH // 2
SHARD = D // NF
F32 = jnp.float32
BF16 = jnp.bfloat16
MIB = 1 << 20


def rcopy(src, dst, send, recv, **where):
    copy = pltpu.make_async_remote_copy(
        src_ref=src,
        dst_ref=dst,
        send_sem=send,
        recv_sem=recv,
        device_id=where,
        device_id_type=pl.DeviceIdType.MESH,
    )
    copy.start()
    return copy


def arrived(ref, sem):
    pltpu.make_async_copy(ref, ref, sem).wait()


def greet():
    f, x = lax.axis_index("fsdp"), lax.axis_index("tensor")
    barrier = pltpu.get_barrier_semaphore()

    def signal(d, carry):
        pl.semaphore_signal(
            barrier,
            inc=1,
            device_id={"fsdp": lax.rem(f + d, NF)},
            device_id_type=pl.DeviceIdType.MESH,
        )
        return carry

    lax.fori_loop(1, NF, signal, 0)
    for d in range(1, NX):
        pl.semaphore_signal(
            barrier,
            inc=1,
            device_id={"tensor": lax.rem(x + d, NX)},
            device_id_type=pl.DeviceIdType.MESH,
        )
    pl.semaphore_wait(barrier, NF - 1 + NX - 1)


def front_kernel(
    hid, gain, w, ids, g,
    xh, wo, emb_o, oh_o, tt_o, pair_o, g_o,
    hid_v, idb, sqb, inv_v, fnd, fet, share,
    loc, id_s, id_r, sq_s, sq_r, a_s, a_r, w_s, w_r, w_r2, x_s, x_r, x_r2, p_s, p_r, m_s, m_r,
):
    f, x = lax.axis_index("fsdp"), lax.axis_index("tensor")
    c = lax.rem(f, 2)
    chip = f // 2
    z, y = lax.rem(chip, 4), chip // 4
    mate = f + 1 - 2 * c
    idx = lambda yy, zz, cc: (yy * 4 + zz) * 2 + cc
    y1, y2, y3 = (lax.rem(y + d, 4) for d in (1, 2, 3))
    z1, z2, z3 = (lax.rem(z + d, 4) for d in (1, 2, 3))
    x1, x2, x3 = (lax.rem(x + d, 4) for d in (1, 2, 3))
    yp, ym, zp, zm = idx(y1, z, c), idx(y3, z, c), idx(y, z1, c), idx(y, z3, c)

    load_hid = pltpu.make_async_copy(hid, hid_v, loc.at[0])
    load_hid.start()
    own_cols = pl.ds(pl.multiple_of(c * HALF, HALF), HALF)
    mate_cols = pl.ds(pl.multiple_of((1 - c) * HALF, HALF), HALF)

    def block(b):
        return wo.at[:, pl.ds(pl.multiple_of(b * SHARD, SHARD), SHARD), :]

    def part(b, h):
        at = pl.multiple_of(b * SHARD + h * (SHARD // 2), SHARD // 2)
        return wo.at[:, pl.ds(at, SHARD // 2), :]

    keep_w = pltpu.make_async_copy(w.at[:, :, own_cols], block(f), loc.at[1])
    keep_w.start()
    keep_id = pltpu.make_async_copy(ids, idb.at[f], loc.at[2])
    keep_id.start()
    keep_g = pltpu.make_async_copy(g.at[:, own_cols], g_o.at[c], loc.at[3])
    keep_g.start()

    greet()

    sends = []
    wcount = [0]

    def wsend(src, dst, recv, dev):
        sends.append(rcopy(src, dst, w_s.at[wcount[0]], recv, fsdp=dev))
        wcount[0] += 1

    def full(b, dev):
        wsend(block(b), block(b), w_r.at[b], dev)

    def half(b, h, dev):
        wsend(part(b, h), part(b, h), (w_r if h == 0 else w_r2).at[b], dev)

    def got(b):
        arrived(block(b), w_r.at[b])

    def got_halves(b):
        arrived(part(b, 0), w_r.at[b])
        arrived(part(b, 1), w_r2.at[b])

    wsend(w.at[:, :, mate_cols], block(f), w_r.at[f], mate)
    for dev in (yp, ym, zp, zm):
        wsend(w.at[:, :, own_cols], block(f), w_r.at[f], dev)

    def id_send(d, carry):
        to = lax.rem(f + d, NF)
        rcopy(ids, idb.at[f], id_s.at[to], id_r.at[f], fsdp=to)
        return carry

    lax.fori_loop(1, NF, id_send, 0)
    sends.append(rcopy(g.at[:, mate_cols], g_o.at[c], m_s, m_r, fsdp=mate))

    load_hid.wait()
    lane = lax.broadcasted_iota(jnp.int32, (128, 128), 1)

    def squares(k, acc):
        v = hid_v[pl.ds(pl.multiple_of(k * 128, 128), 128), :].astype(F32)
        return jnp.where(lane == k, jnp.sum(v * v, axis=1, keepdims=True), acc)

    sqb[x] = lax.fori_loop(0, 16, squares, jnp.zeros((128, 128), F32))
    for n, to in enumerate((x1, x3, x2)):
        sends.append(rcopy(sqb.at[x], sqb.at[x], sq_s.at[n], sq_r.at[x], tensor=to))

    got(mate)
    for dev in (yp, ym, zp, zm):
        full(mate, dev)

    def id_wait(d, carry):
        frm = lax.rem(f + d, NF)
        arrived(idb.at[frm], id_r.at[frm])
        return carry

    lax.fori_loop(1, NF, id_wait, 0)
    keep_id.wait()
    pair_o[c] = idb[f]
    pair_o[1 - c] = idb[mate]
    row = lax.broadcasted_iota(jnp.int32, (SLOTS, ROWS), 0)
    col = lax.broadcasted_iota(jnp.int32, (SLOTS, ROWS), 1)
    slot = lax.rem(row, CAP).astype(F32)
    group = row // CAP
    before = (
        lax.broadcasted_iota(jnp.int32, (ROWS, ROWS), 0) < lax.broadcasted_iota(jnp.int32, (ROWS, ROWS), 1)
    ).astype(F32).astype(BF16)

    def slots_of(named):
        rank = jnp.dot(named.astype(F32).astype(BF16), before, preferred_element_type=F32)
        return named & (rank == slot)

    mine_owner = jnp.broadcast_to(idb[f, 0:1, :], (SLOTS, ROWS))
    tt_o[...] = slots_of(mine_owner == group).astype(F32).astype(BF16)
    table = idb[...].reshape(NF * 8, ROWS).astype(F32).astype(BF16)
    pick_owner = (col == group * 8).astype(F32).astype(BF16)
    pick_item = (col == group * 8 + 1).astype(F32).astype(BF16)
    owner_all = jnp.dot(pick_owner, table, preferred_element_type=F32)
    item_all = jnp.dot(pick_item, table, preferred_element_type=F32)
    taken = slots_of(owner_all == f.astype(F32))
    wanted = jnp.sum(jnp.where(taken, item_all + 1.0, 0.0), axis=1, keepdims=True) - 1.0
    oh_o[...] = (wanted == col.astype(F32)).astype(F32).astype(BF16)

    for frm in (x1, x3, x2):
        arrived(sqb.at[frm], sq_r.at[frm])
    inv_v[...] = lax.rsqrt((sqb[0] + sqb[1] + sqb[2] + sqb[3]) / D + EPSILON)

    def pool(k, carry):
        v = hid_v[pl.ds(pl.multiple_of(k * 128, 128), 128), :].astype(F32)
        inv = jnp.sum(jnp.where(lane == k, inv_v[...], 0.0), axis=1, keepdims=True)
        total = jnp.sum((v * inv).reshape(16, ITEM_LEN, WIDTH), axis=1)
        emb_o[pl.ds(pl.multiple_of(k * 16, 16), 16), :] = (
            total * (1.0 / ITEM_LEN) * gain[...]
        ).astype(BF16)
        return carry

    lax.fori_loop(0, 16, pool, 0)
    fnd[...] = jnp.dot(oh_o[...], emb_o[...], preferred_element_type=F32).astype(BF16)

    def slot_rows(b):
        return pl.ds(pl.multiple_of(b * CAP, CAP), CAP)

    def a_send(d, carry):
        to = lax.rem(f + d, NF)
        rcopy(fnd.at[slot_rows(to)], fet.at[slot_rows(f)], a_s.at[to], a_r.at[f], fsdp=to)
        return carry

    lax.fori_loop(1, NF, a_send, 0)
    fet[slot_rows(f), :] = fnd[slot_rows(f), :]

    for r, prev, nxt, dn, up in ((0, idx(y3, z, 0), idx(y1, z, 0), ym, yp), (1, idx(y, z3, 1), idx(y, z1, 1), zm, zp)):
        got(prev)
        half(prev, 0, up)
        got(nxt)
        half(nxt, 1, dn)
    for dev in (zp, zm):
        full(idx(y3, z, 0), dev)
        full(idx(y1, z, 0), dev)
    for dev in (yp, ym):
        full(idx(y, z3, 1), dev)
        full(idx(y, z1, 1), dev)
    got_halves(idx(y2, z, 0))
    for dev in (zp, zm):
        full(idx(y2, z, 0), dev)
    got_halves(idx(y, z2, 1))
    for dev in (yp, ym):
        full(idx(y, z2, 1), dev)

    def a_wait(d, carry):
        frm = lax.rem(f + d, NF)
        arrived(fet.at[slot_rows(frm)], a_r.at[frm])
        return carry

    lax.fori_loop(1, NF, a_wait, 0)
    share[...] = lax.dot_general(
        tt_o[...], fet[...], (((0,), (0,)), ((), ())), preferred_element_type=F32
    ).astype(BF16)

    def cols(j):
        return pl.ds(pl.multiple_of(j * WIDTH, WIDTH), WIDTH)

    def piece(j, h):
        return xh.at[c, pl.ds(h * (ROWS // 2), ROWS // 2), cols(j)]

    keep_x = pltpu.make_async_copy(share, xh.at[c, :, cols(x)], loc.at[4])
    keep_x.start()
    sends.append(rcopy(share, xh.at[c, :, cols(x)], x_s.at[0], x_r.at[x], tensor=x1))
    sends.append(rcopy(share, xh.at[c, :, cols(x)], x_s.at[1], x_r.at[x], tensor=x3))
    sends.append(rcopy(share, xh.at[c, :, cols(x)], p_s.at[0], p_r.at[x], fsdp=mate))

    for n, (yy, zz) in enumerate(zip((y, y3, y1, y2), (z, z3, z1, z2))):
        got(idx(yy, z3, 0))
        half(idx(yy, z3, 0), 0, zp)
        got(idx(yy, z1, 0))
        half(idx(yy, z1, 0), 1, zm)
        got(idx(y3, zz, 1))
        half(idx(y3, zz, 1), 0, yp)
        got(idx(y1, zz, 1))
        half(idx(y1, zz, 1), 1, ym)
        if n == 0:
            for h, (frm, to) in enumerate(((x3, x1), (x1, x3))):
                arrived(xh.at[c, :, cols(frm)], x_r.at[frm])
                recv = (x_r if h == 0 else x_r2).at[frm]
                sends.append(rcopy(piece(frm, h), piece(frm, h), x_s.at[2 + h], recv, tensor=to))
                whole = xh.at[c, :, cols(frm)]
                sends.append(rcopy(whole, whole, p_s.at[1 + h], p_r.at[frm], fsdp=mate))

    arrived(piece(x2, 0), x_r.at[x2])
    arrived(piece(x2, 1), x_r2.at[x2])
    whole = xh.at[c, :, cols(x2)]
    sends.append(rcopy(whole, whole, p_s.at[3], p_r.at[x2], fsdp=mate))
    for j in (x, x3, x1, x2):
        arrived(xh.at[1 - c, :, cols(j)], p_r.at[j])
    keep_x.wait()

    for yy in (y, y1, y2, y3):
        got_halves(idx(yy, z2, 0))
    for zz in (z, z1, z2, z3):
        got_halves(idx(y2, zz, 1))
    arrived(g_o.at[1 - c], m_r)
    keep_w.wait()
    keep_g.wait()
    for copy in sends:
        copy.wait_send()

    def settle(d, carry):
        to = lax.rem(f + d, NF)
        pltpu.make_async_copy(ids, ids, id_s.at[to]).wait()
        pltpu.make_async_copy(fnd.at[slot_rows(to)], fnd.at[slot_rows(to)], a_s.at[to]).wait()
        return carry

    lax.fori_loop(1, NF, settle, 0)


ANY = pl.BlockSpec(memory_space=pl.ANY)
VMEM = pl.BlockSpec(memory_space=pltpu.VMEM)
DMA = pltpu.SemaphoreType.DMA


def front(item_hidden, item_gain, wqkv, ids, grad_out):
    return pl.pallas_call(
        front_kernel,
        out_shape=(
            jax.ShapeDtypeStruct((2, ROWS, D), BF16),
            jax.ShapeDtypeStruct((3, D, HALF), BF16),
            jax.ShapeDtypeStruct((ROWS, WIDTH), BF16),
            jax.ShapeDtypeStruct((SLOTS, ROWS), BF16),
            jax.ShapeDtypeStruct((SLOTS, ROWS), BF16),
            jax.ShapeDtypeStruct((2, 8, ROWS), jnp.int32),
            jax.ShapeDtypeStruct((2, ROWS, HALF), BF16),
        ),
        in_specs=[ANY, VMEM, ANY, ANY, ANY],
        out_specs=(ANY, ANY, VMEM, VMEM, VMEM, VMEM, ANY),
        scratch_shapes=[
            pltpu.VMEM((ROWS * ITEM_LEN, WIDTH), BF16),
            pltpu.VMEM((NF, 8, ROWS), jnp.int32),
            pltpu.VMEM((NX, 128, 128), F32),
            pltpu.VMEM((128, 128), F32),
            pltpu.VMEM((SLOTS, WIDTH), BF16),
            pltpu.VMEM((SLOTS, WIDTH), BF16),
            pltpu.VMEM((ROWS, WIDTH), BF16),
            DMA((5,)),
            DMA((NF,)), DMA((NF,)),
            DMA((3,)), DMA((NX,)),
            DMA((NF,)), DMA((NF,)),
            DMA((41,)), DMA((NF,)), DMA((NF,)),
            DMA((4,)), DMA((NX,)), DMA((NX,)),
            DMA((4,)), DMA((NX,)),
            DMA, DMA,
        ],
        compiler_params=pltpu.CompilerParams(
            collective_id=0, has_side_effects=True, vmem_limit_bytes=48 * MIB
        ),
        cost_estimate=pl.CostEstimate(flops=10**9, bytes_accessed=64 * MIB, transcendentals=0),
        name="front",
    )(item_hidden, item_gain, wqkv, ids, grad_out)


def core_kernel(
    xh, gain, pair, g, w,
    attn, dx, inv_o, stat,
    wv, nrm, acc, qkv, grads, sem,
):
    loads = [pltpu.make_async_copy(w.at[n], wv.at[n], sem.at[n]) for n in range(3)]
    for load in loads:
        load.start()

    def norm(k, carry):
        rows = pl.ds(pl.multiple_of(k * 32, 32), 32)
        v = xh[rows, :].astype(F32)
        inv = lax.rsqrt(jnp.sum(v * v, axis=1, keepdims=True) / D + EPSILON)
        nrm[rows, :] = (v * inv * gain[...]).astype(BF16)
        inv_o[rows, :] = jnp.broadcast_to(inv, (32, 128))
        return carry

    lax.fori_loop(0, 16, norm, 0)

    steps = 4
    depth = D // steps
    for n in range(3):
        loads[n].wait()

        def project(k, carry):
            at = pl.ds(pl.multiple_of(k * depth, depth), depth)
            acc[...] += jnp.dot(nrm[:, at], wv[n, at, :], preferred_element_type=F32)
            return carry

        acc[...] = jnp.zeros_like(acc)
        lax.fori_loop(0, steps, project, 0)
        qkv[n] = acc[...].astype(BF16)

    factor = 1.0 / math.sqrt(HEAD_DIM)
    heads = HALF // HEAD_DIM
    t_at = lax.broadcasted_iota(jnp.int32, (ROWS, ROWS), 0)
    s_at = lax.broadcasted_iota(jnp.int32, (ROWS, ROWS), 1)
    t_row = lax.broadcasted_iota(jnp.int32, (ROWS, HEAD_DIM), 0)
    nt = (((1,), (1,)), ((), ()))
    tn = (((0,), (0,)), ((), ()))

    def attend(k, carry):
        h, n = k // heads, lax.rem(k, heads)
        rows = pl.ds(pl.multiple_of(h * ROWS, ROWS), ROWS)
        cols = pl.ds(pl.multiple_of(n * HEAD_DIM, HEAD_DIM), HEAD_DIM)
        length = pair[h, 2:3, :]
        allowed = (s_at <= t_at) & (s_at < length)
        live = t_row < length[:, :HEAD_DIM]
        qq, kk, vv = qkv[0, rows, cols], qkv[1, rows, cols], qkv[2, rows, cols]
        gg = jnp.where(live, g[h, :, cols].astype(F32), 0.0).astype(BF16)
        scores = lax.dot_general(qq, kk, nt, preferred_element_type=F32) * factor
        scores = jnp.where(allowed, scores, -1e30)
        top = jnp.max(scores, axis=1, keepdims=True)
        raised = jnp.where(allowed, jnp.exp(scores - top), 0.0)
        probs = raised * (1.0 / jnp.sum(raised, axis=1, keepdims=True))
        pb = probs.astype(BF16)
        out = jnp.dot(pb, vv, preferred_element_type=F32)
        attn[rows, cols] = jnp.where(live, out, 0.0).astype(BF16)
        dv = lax.dot_general(pb, gg, tn, preferred_element_type=F32).astype(BF16)
        dp = lax.dot_general(gg, vv, nt, preferred_element_type=F32)
        mid = jnp.sum(probs * dp, axis=1, keepdims=True)
        ds = (probs * (dp - mid) * factor).astype(BF16)
        dq = jnp.dot(ds, kk, preferred_element_type=F32).astype(BF16)
        dk = lax.dot_general(ds, qq, tn, preferred_element_type=F32).astype(BF16)
        grads[0, rows, cols] = dq
        grads[1, rows, cols] = dk
        grads[2, rows, cols] = dv
        terms = (
            dq.astype(F32) * qq.astype(F32)
            + dk.astype(F32) * kk.astype(F32)
            + dv.astype(F32) * vv.astype(F32)
        )
        stat[rows, :] += jnp.broadcast_to(jnp.sum(terms, axis=1, keepdims=True), (ROWS, 128))
        return carry

    stat[...] = jnp.zeros_like(stat)
    lax.fori_loop(0, 2 * heads, attend, 0)

    def back(k, carry):
        at = pl.ds(pl.multiple_of(k * 512, 512), 512)
        total = jnp.zeros((2 * ROWS, 512), F32)
        for n in range(3):
            total += lax.dot_general(grads[n], wv[n, at, :], nt, preferred_element_type=F32)
        dx[:, at] = total.astype(BF16)
        return carry

    lax.fori_loop(0, D // 512, back, 0)


def core(xh, gain, pair, g, w):
    rows = 2 * ROWS
    return pl.pallas_call(
        core_kernel,
        out_shape=(
            jax.ShapeDtypeStruct((rows, HALF), BF16),
            jax.ShapeDtypeStruct((rows, D), BF16),
            jax.ShapeDtypeStruct((rows, 128), F32),
            jax.ShapeDtypeStruct((rows, 128), F32),
        ),
        in_specs=[VMEM, VMEM, VMEM, VMEM, ANY],
        out_specs=(VMEM,) * 4,
        scratch_shapes=[
            pltpu.VMEM((3, D, HALF), BF16),
            pltpu.VMEM((rows, D), BF16),
            pltpu.VMEM((rows, HALF), F32),
            pltpu.VMEM((3, rows, HALF), BF16),
            pltpu.VMEM((3, rows, HALF), BF16),
            DMA((3,)),
        ],
        compiler_params=pltpu.CompilerParams(vmem_limit_bytes=56 * MIB),
        cost_estimate=pl.CostEstimate(flops=26 * 10**9, bytes_accessed=24 * MIB, transcendentals=10**6),
        name="core",
    )(xh, gain, pair, g, w)


def tail_kernel(
    dx, stat, inv, xh, gain, tt, attn,
    inc, attn_o,
    mine, cbuf, pbuf, rdir, rfwd, sbuf, xv, og,
    loc, c_s, c_r, x_s, x_r, st_s, st_r, a_s, a_r, m_s, m_r,
):
    f, x = lax.axis_index("fsdp"), lax.axis_index("tensor")
    c = lax.rem(f, 2)
    mate = f + 1 - 2 * c
    x1, x2, x3 = (lax.rem(x + d, 4) for d in (1, 2, 3))
    low, high = pl.ds(0, ROWS // 2), pl.ds(ROWS // 2, ROWS // 2)

    def cols(j):
        return pl.ds(pl.multiple_of(j * WIDTH, WIDTH), WIDTH)

    rows_own = pl.ds(pl.multiple_of(c * ROWS, ROWS), ROWS)
    rows_mate = pl.ds(pl.multiple_of((1 - c) * ROWS, ROWS), ROWS)
    head_cols = pl.ds(pl.multiple_of(c * HALF, HALF), HALF)
    order = (x2, x1, x3, x)
    load_x = pltpu.make_async_copy(xh.at[c, :, cols(x)], xv, loc.at[0])
    load_x.start()
    keep_a = pltpu.make_async_copy(attn.at[rows_own], attn_o.at[:, head_cols], loc.at[1])
    keep_a.start()
    load_d = []
    for n, j in enumerate(order):
        load_d.append(pltpu.make_async_copy(dx.at[rows_own, cols(j)], mine.at[n], loc.at[2 + n]))
        load_d[-1].start()
    greet()
    sends = []
    for n, j in enumerate(order):
        sends.append(rcopy(dx.at[rows_mate, cols(j)], cbuf.at[n], c_s.at[n], c_r.at[n], fsdp=mate))
    sends.append(rcopy(stat.at[rows_mate], sbuf.at[4], st_s.at[3], st_r.at[4], fsdp=mate))
    sends.append(rcopy(attn.at[rows_mate], attn_o.at[:, head_cols], m_s, m_r, fsdp=mate))

    def summed(n):
        arrived(cbuf.at[n], c_r.at[n])
        load_d[n].wait()
        return mine[n].astype(F32) + cbuf[n].astype(F32)

    pbuf[0] = summed(0).astype(BF16)
    sends.append(rcopy(pbuf.at[0, low], rfwd.at[0], x_s.at[0], x_r.at[0], tensor=x1))
    sends.append(rcopy(pbuf.at[0, high], rfwd.at[1], x_s.at[1], x_r.at[1], tensor=x3))
    pbuf[1] = summed(1).astype(BF16)
    sends.append(rcopy(pbuf.at[1, high], rdir.at[0, high], x_s.at[2], x_r.at[2], tensor=x1))
    pbuf[2] = summed(2).astype(BF16)
    sends.append(rcopy(pbuf.at[2, low], rdir.at[1, low], x_s.at[3], x_r.at[3], tensor=x3))
    arrived(sbuf.at[4], st_r.at[4])
    sbuf[x] = stat[rows_own, :] + sbuf[4]
    for n, to in enumerate((x1, x3, x2)):
        sends.append(rcopy(sbuf.at[x], sbuf.at[x], st_s.at[n], st_r.at[x], tensor=to))
    arrived(rfwd.at[0], x_r.at[0])
    pbuf[1, low, :] = (pbuf[1, low, :].astype(F32) + rfwd[0].astype(F32)).astype(BF16)
    sends.append(rcopy(pbuf.at[1, low], rdir.at[0, low], x_s.at[4], x_r.at[4], tensor=x1))
    arrived(rfwd.at[1], x_r.at[1])
    pbuf[2, high, :] = (pbuf[2, high, :].astype(F32) + rfwd[1].astype(F32)).astype(BF16)
    sends.append(rcopy(pbuf.at[2, high], rdir.at[1, high], x_s.at[5], x_r.at[5], tensor=x3))
    pbuf[3] = summed(3).astype(BF16)
    for frm in (x1, x3, x2):
        arrived(sbuf.at[frm], st_r.at[frm])
    load_x.wait()
    arrived(rdir.at[0, high], x_r.at[2])
    arrived(rdir.at[1, low], x_r.at[3])
    arrived(rdir.at[0, low], x_r.at[4])
    arrived(rdir.at[1, high], x_r.at[5])
    iv = inv[rows_own, 0:1]
    total = (sbuf[0] + sbuf[1] + sbuf[2] + sbuf[3])[:, 0:1]
    coef = iv * iv * total / D
    summed_all = pbuf[3].astype(F32) + rdir[0].astype(F32) + rdir[1].astype(F32)
    grad = iv * (summed_all * gain[:, cols(x)]) - xv[...].astype(F32) * coef
    og[...] = jnp.dot(tt[...], grad.astype(BF16), preferred_element_type=F32).astype(BF16)

    def slot_rows(b):
        return pl.ds(pl.multiple_of(b * CAP, CAP), CAP)

    def a_send(d, carry):
        to = lax.rem(f + d, NF)
        rcopy(og.at[slot_rows(to)], inc.at[slot_rows(f)], a_s.at[to], a_r.at[f], fsdp=to)
        return carry

    lax.fori_loop(1, NF, a_send, 0)
    keep_o = pltpu.make_async_copy(og.at[slot_rows(f)], inc.at[slot_rows(f)], loc.at[6])
    keep_o.start()

    def a_wait(d, carry):
        frm = lax.rem(f + d, NF)
        arrived(inc.at[slot_rows(frm)], a_r.at[frm])
        arrived(og.at[slot_rows(frm)], a_s.at[frm])
        return carry

    lax.fori_loop(1, NF, a_wait, 0)
    keep_o.wait()
    keep_a.wait()
    mate_head = pl.ds(pl.multiple_of((1 - c) * HALF, HALF), HALF)
    arrived(attn_o.at[:, mate_head], m_r)
    for copy in sends:
        copy.wait_send()


def tail(dx, stat, inv, xh, gain, tt, attn):
    block = pltpu.VMEM((4, ROWS, WIDTH), BF16)
    return pl.pallas_call(
        tail_kernel,
        out_shape=(
            jax.ShapeDtypeStruct((SLOTS, WIDTH), BF16),
            jax.ShapeDtypeStruct((ROWS, WIDTH), BF16),
        ),
        in_specs=[ANY, VMEM, VMEM, ANY, VMEM, VMEM, ANY],
        out_specs=(ANY, ANY),
        scratch_shapes=[
            block,
            block,
            block,
            pltpu.VMEM((2, ROWS, WIDTH), BF16),
            pltpu.VMEM((2, ROWS // 2, WIDTH), BF16),
            pltpu.VMEM((5, ROWS, 128), F32),
            pltpu.VMEM((ROWS, WIDTH), BF16),
            pltpu.VMEM((SLOTS, WIDTH), BF16),
            DMA((7,)),
            DMA((4,)), DMA((4,)),
            DMA((6,)), DMA((6,)),
            DMA((4,)), DMA((5,)),
            DMA((NF,)), DMA((NF,)),
            DMA, DMA,
        ],
        compiler_params=pltpu.CompilerParams(
            collective_id=1, has_side_effects=True, vmem_limit_bytes=48 * MIB
        ),
        cost_estimate=pl.CostEstimate(flops=10**9, bytes_accessed=16 * MIB, transcendentals=0),
        name="tail",
    )(dx, stat, inv, xh, gain, tt, attn)


def on_device(item_hidden, item_gain, occ_owner, occ_item, hist_len, user_gain, wqkv, grad_out):
    ids = jnp.stack(
        [occ_owner[:, 0], occ_item, jnp.broadcast_to(hist_len, (ROWS,))]
        + [jnp.zeros((ROWS,), jnp.int32)] * 5
    )
    gain = user_gain.reshape(1, D)
    xh, w, item_embed, wanted, placed, pair, g = front(
        item_hidden, item_gain.reshape(1, WIDTH), wqkv, ids, grad_out
    )
    attn, dx, inv, stat = core(xh.reshape(2 * ROWS, D), gain, pair, g, w)
    incoming, attended = tail(dx, stat, inv, xh, gain, placed, attn)
    item_grads = lax.dot_general(
        wanted, incoming, (((0,), (0,)), ((), ())), preferred_element_type=F32
    )
    return (item_embed, attended, item_grads)


def solution(mesh):
    in_specs = (
        P("fsdp", "tensor"),
        P("tensor"),
        P("fsdp", None),
        P("fsdp"),
        P("fsdp"),
        P(),
        P(None, "fsdp", "tensor"),
        P("fsdp", "tensor"),
    )
    out_specs = (P("fsdp", "tensor"), P("fsdp", "tensor"), P("fsdp", "tensor"))
    return jax.shard_map(
        on_device, mesh=mesh, in_specs=in_specs, out_specs=out_specs, check_vma=False
    )
```

```python
import functools
import math

import jax
import jax.numpy as jnp
from jax import lax
from jax.experimental import pallas as pl
from jax.experimental.pallas import tpu as pltpu
from jax.sharding import PartitionSpec as P

D = 4096
HEAD_DIM = 128
ITEM_LEN = 8
EPSILON = 1e-05
NF = 32
NX = 4
ROWS = 256
CAP = 16
SLOTS = NF * CAP
WIDTH = D // NX
HALF = WIDTH // 2
SHARD = D // NF
GROUP = HALF // 2
TRIO = 3 * GROUP
UNIT = WIDTH // 2
ALL3 = 2 * TRIO
BOTH = 2 * ROWS
F32 = jnp.float32
BF16 = jnp.bfloat16
MIB = 1 << 20


def rcopy(src, dst, send, recv, **where):
    copy = pltpu.make_async_remote_copy(
        src_ref=src,
        dst_ref=dst,
        send_sem=send,
        recv_sem=recv,
        device_id=where,
        device_id_type=pl.DeviceIdType.MESH,
    )
    copy.start()
    return copy


def arrived(ref, sem):
    pltpu.make_async_copy(ref, ref, sem).wait()


def greet():
    f, x = lax.axis_index("fsdp"), lax.axis_index("tensor")
    barrier = pltpu.get_barrier_semaphore()

    def signal(d, carry):
        pl.semaphore_signal(
            barrier,
            inc=1,
            device_id={"fsdp": lax.rem(f + d, NF)},
            device_id_type=pl.DeviceIdType.MESH,
        )
        return carry

    lax.fori_loop(1, NF, signal, 0)
    for d in range(1, NX):
        pl.semaphore_signal(
            barrier,
            inc=1,
            device_id={"tensor": lax.rem(x + d, NX)},
            device_id_type=pl.DeviceIdType.MESH,
        )
    pl.semaphore_wait(barrier, NF - 1 + NX - 1)


def layer_kernel(
    hid, gain, w, ids, g, ugain,
    emb_o, oh_o, attn_o, inc,
    hid_v, idb, sqb, inv_v, tt, fnd, fet, share,
    wv, xh, nrm, acc, qkv, grads, gv, attn, inv_h, stat, sbuf,
    dxs, cbuf, pbuf, rdir, rfwd, og,
    loc, id_s, id_r, sq_s, sq_r, a_s, a_r, w_s, w_r, wm_s, wm_r,
    x_s, x_r, p_s, p_r, g_s, g_r, at_s, at_r, st_s, st_r,
    c_s, c_r, r_s, r_r, b_s, b_r,
):
    f, x = lax.axis_index("fsdp"), lax.axis_index("tensor")
    c = lax.rem(f, 2)
    chip = f // 2
    z, y = lax.rem(chip, 4), chip // 4
    mate = f + 1 - 2 * c
    y1, y2, y3 = (lax.rem(y + d, 4) for d in (1, 2, 3))
    z1, z2, z3 = (lax.rem(z + d, 4) for d in (1, 2, 3))
    x1, x2, x3 = (lax.rem(x + d, 4) for d in (1, 2, 3))
    at_chip = lambda yy, zz: yy * 4 + zz
    yp, ym = at_chip(y1, z) * 2 + c, at_chip(y3, z) * 2 + c
    zp, zm = at_chip(y, z1) * 2 + c, at_chip(y, z3) * 2 + c
    sends = []

    def ds(i, n):
        return pl.ds(pl.multiple_of(i * n, n), n)

    load_hid = pltpu.make_async_copy(hid, hid_v, loc.at[0])
    load_hid.start()
    keep_w = []
    for h in range(2):
        for n in range(3):
            src = w.at[n, :, pl.ds(pl.multiple_of(c * HALF + h * GROUP, GROUP), GROUP)]
            dst = wv.at[ds(f, SHARD), pl.ds(h * TRIO + n * GROUP, GROUP)]
            keep_w.append(pltpu.make_async_copy(src, dst, loc.at[4 + h * 3 + n]))
            keep_w[-1].start()
    keep_id = pltpu.make_async_copy(ids, idb.at[f], loc.at[1])
    keep_id.start()
    keep_g = pltpu.make_async_copy(g.at[:, ds(c, HALF)], gv.at[c], loc.at[2])
    keep_g.start()
    greet()

    def piece(h, s):
        return wv.at[ds(s, SHARD), pl.ds(h * TRIO, TRIO)]

    wcount = [0]

    def wsend(h, s, dev):
        sends.append(rcopy(piece(h, s), piece(h, s), w_s.at[wcount[0]], w_r.at[h * NF + s], fsdp=dev))
        wcount[0] += 1

    def got(h, s):
        arrived(piece(h, s), w_r.at[h * NF + s])

    for h in range(2):
        for n in range(3):
            src = w.at[n, :, pl.ds(pl.multiple_of((1 - c) * HALF + h * GROUP, GROUP), GROUP)]
            dst = wv.at[ds(f, SHARD), pl.ds(h * TRIO + n * GROUP, GROUP)]
            sends.append(rcopy(src, dst, wm_s.at[h * 3 + n], wm_r.at[h * 3 + n], fsdp=mate))
    for h in range(2):
        for copy in keep_w[3 * h : 3 * h + 3]:
            copy.wait()
        for dev in (yp, ym, zp, zm) if h == 0 else (zp, zm, yp, ym):
            wsend(h, f, dev)

    def id_send(d, carry):
        to = lax.rem(f + d, NF)
        rcopy(ids, idb.at[f], id_s.at[to], id_r.at[f], fsdp=to)
        return carry

    lax.fori_loop(1, NF, id_send, 0)
    sends.append(rcopy(g.at[:, ds(1 - c, HALF)], gv.at[c], g_s, g_r, fsdp=mate))

    load_hid.wait()
    lane = lax.broadcasted_iota(jnp.int32, (128, 128), 1)

    def squares(k, total):
        v = hid_v[ds(k, 128), :].astype(F32)
        return jnp.where(lane == k, jnp.sum(v * v, axis=1, keepdims=True), total)

    sqb[x] = lax.fori_loop(0, 16, squares, jnp.zeros((128, 128), F32))
    for n, to in enumerate((x1, x3, x2)):
        sends.append(rcopy(sqb.at[x], sqb.at[x], sq_s.at[n], sq_r.at[x], tensor=to))

    for h in range(2):
        for n in range(3):
            dst = wv.at[ds(mate, SHARD), pl.ds(h * TRIO + n * GROUP, GROUP)]
            arrived(dst, wm_r.at[h * 3 + n])
        for dev in (yp, ym, zp, zm) if h == 0 else (zp, zm, yp, ym):
            wsend(h, mate, dev)

    def id_wait(d, carry):
        frm = lax.rem(f + d, NF)
        arrived(idb.at[frm], id_r.at[frm])
        return carry

    lax.fori_loop(1, NF, id_wait, 0)
    keep_id.wait()
    row = lax.broadcasted_iota(jnp.int32, (SLOTS, ROWS), 0)
    col = lax.broadcasted_iota(jnp.int32, (SLOTS, ROWS), 1)
    slot = lax.rem(row, CAP).astype(F32)
    group = row // CAP
    t_at = lax.broadcasted_iota(jnp.int32, (ROWS, ROWS), 0)
    s_at = lax.broadcasted_iota(jnp.int32, (ROWS, ROWS), 1)
    before = (t_at < s_at).astype(F32).astype(BF16)

    def slots_of(named):
        rank = jnp.dot(named.astype(F32).astype(BF16), before, preferred_element_type=F32)
        return named & (rank == slot)

    mine_owner = jnp.broadcast_to(idb[f, 0:1, :], (SLOTS, ROWS))
    tt[...] = slots_of(mine_owner == group).astype(F32).astype(BF16)
    table = idb[...].reshape(NF * 8, ROWS).astype(F32).astype(BF16)
    pick_owner = (col == group * 8).astype(F32).astype(BF16)
    pick_item = (col == group * 8 + 1).astype(F32).astype(BF16)
    owner_all = jnp.dot(pick_owner, table, preferred_element_type=F32)
    item_all = jnp.dot(pick_item, table, preferred_element_type=F32)
    taken = slots_of(owner_all == f.astype(F32))
    wanted = jnp.sum(jnp.where(taken, item_all + 1.0, 0.0), axis=1, keepdims=True) - 1.0
    oh_o[...] = (wanted == col.astype(F32)).astype(F32).astype(BF16)

    for frm in (x1, x3, x2):
        arrived(sqb.at[frm], sq_r.at[frm])
    inv_v[...] = lax.rsqrt((sqb[0] + sqb[1] + sqb[2] + sqb[3]) / D + EPSILON)

    def pool(k, carry):
        v = hid_v[ds(k, 128), :].astype(F32)
        inv = jnp.sum(jnp.where(lane == k, inv_v[...], 0.0), axis=1, keepdims=True)
        total = jnp.sum((v * inv).reshape(16, ITEM_LEN, WIDTH), axis=1)
        emb_o[ds(k, 16), :] = (total * (1.0 / ITEM_LEN) * gain[...]).astype(BF16)
        return carry

    lax.fori_loop(0, 16, pool, 0)
    fnd[...] = jnp.dot(oh_o[...], emb_o[...], preferred_element_type=F32).astype(BF16)

    def a_send(d, carry):
        to = lax.rem(f + d, NF)
        rcopy(fnd.at[ds(to, CAP)], fet.at[ds(f, CAP)], a_s.at[to], a_r.at[f], fsdp=to)
        return carry

    lax.fori_loop(1, NF, a_send, 0)
    fet[ds(f, CAP), :] = fnd[ds(f, CAP), :]

    prev = (at_chip(y3, z), at_chip(y, z3))
    nxt = (at_chip(y1, z), at_chip(y, z1))
    far = (at_chip(y2, z), at_chip(y, z2))
    ways = ((yp, ym), (zp, zm))
    for h in range(2):
        up, dn = ways[h]
        got(h, prev[h] * 2)
        wsend(h, prev[h] * 2, up)
        got(h, nxt[h] * 2 + 1)
        wsend(h, nxt[h] * 2 + 1, dn)
    for h in range(2):
        got(h, prev[h] * 2 + 1)
        got(h, nxt[h] * 2)
        for s in (prev[h] * 2, nxt[h] * 2 + 1, prev[h] * 2 + 1, nxt[h] * 2):
            for dev in ways[1 - h]:
                wsend(h, s, dev)
    for h in range(2):
        for r in range(2):
            got(h, far[h] * 2 + r)
            for dev in ways[1 - h]:
                wsend(h, far[h] * 2 + r, dev)

    def a_wait(d, carry):
        frm = lax.rem(f + d, NF)
        arrived(fet.at[ds(frm, CAP)], a_r.at[frm])
        return carry

    lax.fori_loop(1, NF, a_wait, 0)
    share[...] = lax.dot_general(
        tt[...], fet[...], (((0,), (0,)), ((), ())), preferred_element_type=F32
    ).astype(BF16)

    def xpart(j, h):
        return xh.at[c, pl.ds(h * (ROWS // 2), ROWS // 2), ds(j, WIDTH)]

    def xwhole(k, j):
        return xh.at[k, :, ds(j, WIDTH)]

    keep_x = pltpu.make_async_copy(share, xwhole(c, x), loc.at[3])
    keep_x.start()
    for h in range(2):
        half = share.at[pl.ds(h * (ROWS // 2), ROWS // 2)]
        sends.append(rcopy(half, xpart(x, h), x_s.at[h], x_r.at[2 * x + h], tensor=x1))
        sends.append(rcopy(half, xpart(x, h), x_s.at[2 + h], x_r.at[2 * x + h], tensor=x3))
    sends.append(rcopy(share, xwhole(c, x), p_s.at[0], p_r.at[x], fsdp=mate))

    def third(n):
        yy, zz = ((y, z), (y3, z3), (y1, z1), (y2, z2))[n]
        from_low = (at_chip(yy, z3), at_chip(y3, zz))
        from_high = (at_chip(yy, z1), at_chip(y1, zz))
        for h in range(2):
            up, dn = ways[1 - h]
            got(h, from_low[h] * 2)
            wsend(h, from_low[h] * 2, up)
            got(h, from_high[h] * 2 + 1)
            wsend(h, from_high[h] * 2 + 1, dn)
        for h in range(2):
            got(h, from_low[h] * 2 + 1)
            got(h, from_high[h] * 2)

    def x_forward():
        for h, (frm, to) in enumerate(((x3, x1), (x1, x3))):
            arrived(xpart(frm, h), x_r.at[2 * frm + h])
            sends.append(rcopy(xpart(frm, h), xpart(frm, h), x_s.at[4 + h], x_r.at[2 * frm + h], tensor=to))
        for h, frm in enumerate((x3, x1)):
            arrived(xpart(frm, 1 - h), x_r.at[2 * frm + 1 - h])
            sends.append(rcopy(xwhole(c, frm), xwhole(c, frm), p_s.at[1 + h], p_r.at[frm], fsdp=mate))

    def x_finish():
        for h in range(2):
            arrived(xpart(x2, h), x_r.at[2 * x2 + h])
        sends.append(rcopy(xwhole(c, x2), xwhole(c, x2), p_s.at[3], p_r.at[x2], fsdp=mate))
        keep_x.wait()

    def norm(k, carry):
        h, m = k // 8, lax.rem(k, 8)
        v = xh[h, ds(m, 32), :].astype(F32)
        inv = lax.rsqrt(jnp.sum(v * v, axis=1, keepdims=True) / D + EPSILON)
        nrm[ds(k, 32), :] = (v * inv * ugain[...]).astype(BF16)
        inv_h[ds(k, 32), :] = jnp.broadcast_to(inv, (32, 128))
        return carry

    third(0)
    x_forward()
    third(1)
    third(2)
    x_finish()
    lax.fori_loop(c * 8, c * 8 + 8, norm, 0)
    third(3)
    for j in (x, x3, x1, x2):
        arrived(xwhole(1 - c, j), p_r.at[j])
    lax.fori_loop((1 - c) * 8, (1 - c) * 8 + 8, norm, 0)

    def project(h, k, depth):
        acc[h] += jnp.dot(
            nrm[:, ds(k, depth)],
            wv[ds(k, depth), h * TRIO : (h + 1) * TRIO],
            preferred_element_type=F32,
        )

    def near_h1(t, carry):
        project(1, lax.rem(y + 3 + t, 4), 1024)
        return carry

    def near_h0(t, carry):
        project(0, at_chip(lax.rem(t, 4), lax.rem(z + 3 + t // 4, 4)), 256)
        return carry

    def far_h0(t, carry):
        project(0, at_chip(t, z2), 256)
        return carry

    acc[...] = jnp.zeros_like(acc)
    lax.fori_loop(0, 3, near_h1, 0)
    lax.fori_loop(0, 12, near_h0, 0)
    for yy in (y, y3, y1, y2):
        for r in range(2):
            got(0, at_chip(yy, z2) * 2 + r)
    lax.fori_loop(0, 4, far_h0, 0)
    qkv[:, 0:TRIO] = acc[0].astype(BF16)
    for zz in (z, z3, z1, z2):
        for r in range(2):
            got(1, at_chip(y2, zz) * 2 + r)
    project(1, y2, 1024)
    qkv[:, TRIO:ALL3] = acc[1].astype(BF16)

    factor = 1.0 / math.sqrt(HEAD_DIM)
    t_row = lax.broadcasted_iota(jnp.int32, (ROWS, HEAD_DIM), 0)
    nt = (((1,), (1,)), ((), ()))
    tn = (((0,), (0,)), ((), ()))
    keep_g.wait()
    arrived(gv.at[1 - c], g_r)

    def attend(k, carry):
        h, n = k // 4, lax.rem(k, 4)
        rows = ds(h, ROWS)
        cols = ds(n, HEAD_DIM)
        base = (n // 2) * TRIO + lax.rem(n, 2) * HEAD_DIM
        q_at, k_at, v_at = (
            pl.ds(pl.multiple_of(base + i * GROUP, HEAD_DIM), HEAD_DIM) for i in range(3)
        )
        length = idb[chip * 2 + h, 2:3, :]
        allowed = (s_at <= t_at) & (s_at < length)
        live = t_row < length[:, :HEAD_DIM]
        qq, kk, vv = qkv[rows, q_at], qkv[rows, k_at], qkv[rows, v_at]
        gg = jnp.where(live, gv[h, :, cols].astype(F32), 0.0).astype(BF16)
        scores = lax.dot_general(qq, kk, nt, preferred_element_type=F32) * factor
        scores = jnp.where(allowed, scores, -1e30)
        top = jnp.max(scores, axis=1, keepdims=True)
        raised = jnp.where(allowed, jnp.exp(scores - top), 0.0)
        probs = raised * (1.0 / jnp.sum(raised, axis=1, keepdims=True))
        pb = probs.astype(BF16)
        out = jnp.dot(pb, vv, preferred_element_type=F32)
        attn[rows, cols] = jnp.where(live, out, 0.0).astype(BF16)
        dv = lax.dot_general(pb, gg, tn, preferred_element_type=F32).astype(BF16)
        dp = lax.dot_general(gg, vv, nt, preferred_element_type=F32)
        mid = jnp.sum(probs * dp, axis=1, keepdims=True)
        dsc = (probs * (dp - mid) * factor).astype(BF16)
        dq = jnp.dot(dsc, kk, preferred_element_type=F32).astype(BF16)
        dk = lax.dot_general(dsc, qq, tn, preferred_element_type=F32).astype(BF16)
        grads[rows, q_at] = dq
        grads[rows, k_at] = dk
        grads[rows, v_at] = dv
        terms = (
            dq.astype(F32) * qq.astype(F32)
            + dk.astype(F32) * kk.astype(F32)
            + dv.astype(F32) * vv.astype(F32)
        )
        stat[rows, :] += jnp.broadcast_to(jnp.sum(terms, axis=1, keepdims=True), (ROWS, 128))
        return carry

    stat[...] = jnp.zeros_like(stat)
    lax.fori_loop(0, 8, attend, 0)

    rows_own, rows_mate = ds(c, ROWS), ds(1 - c, ROWS)
    low, high = pl.ds(0, ROWS // 2), pl.ds(ROWS // 2, ROWS // 2)
    sends.append(rcopy(stat.at[rows_mate], sbuf.at[4], st_s.at[3], st_r.at[4], fsdp=mate))
    order = (x2, x1, x3, x)

    def back(u):
        q, n = u // 4, u % 4
        at = pl.ds(pl.multiple_of(order[n] * WIDTH + q * UNIT, UNIT), UNIT)
        dxs[u] = lax.dot_general(grads[...], wv[at, :], nt, preferred_element_type=F32).astype(BF16)
        sends.append(rcopy(dxs.at[u, rows_mate], cbuf.at[u], c_s.at[u], c_r.at[u], fsdp=mate))

    def summed(u):
        arrived(cbuf.at[u], c_r.at[u])
        pbuf[u] = (dxs[u, rows_own, :].astype(F32) + cbuf[u].astype(F32)).astype(BF16)

    def ring(q, k, src, dst, to):
        sends.append(rcopy(src, dst, r_s.at[q * 6 + k], r_r.at[q * 6 + k], tensor=to))

    def far_out(q):
        summed(q * 4)
        ring(q, 0, pbuf.at[q * 4, low], rfwd.at[q, 0], x1)
        ring(q, 1, pbuf.at[q * 4, high], rfwd.at[q, 1], x3)

    def near_out(q):
        summed(q * 4 + 1)
        ring(q, 2, pbuf.at[q * 4 + 1, high], rdir.at[q, 0, high], x1)
        summed(q * 4 + 2)
        ring(q, 3, pbuf.at[q * 4 + 2, low], rdir.at[q, 1, low], x3)

    def add_out(q):
        arrived(rfwd.at[q, 0], r_r.at[q * 6])
        u = q * 4 + 1
        pbuf[u, low, :] = (pbuf[u, low, :].astype(F32) + rfwd[q, 0].astype(F32)).astype(BF16)
        ring(q, 4, pbuf.at[u, low], rdir.at[q, 0, low], x1)
        arrived(rfwd.at[q, 1], r_r.at[q * 6 + 1])
        u = q * 4 + 2
        pbuf[u, high, :] = (pbuf[u, high, :].astype(F32) + rfwd[q, 1].astype(F32)).astype(BF16)
        ring(q, 5, pbuf.at[u, high], rdir.at[q, 1, high], x3)

    def a_out(q):
        arrived(rdir.at[q, 0, high], r_r.at[q * 6 + 2])
        arrived(rdir.at[q, 1, low], r_r.at[q * 6 + 3])
        arrived(rdir.at[q, 0, low], r_r.at[q * 6 + 4])
        arrived(rdir.at[q, 1, high], r_r.at[q * 6 + 5])
        iv = inv_h[rows_own, 0:1]
        total = (sbuf[0] + sbuf[1] + sbuf[2] + sbuf[3])[:, 0:1]
        coef = iv * iv * total / D
        at = pl.ds(pl.multiple_of(x * WIDTH + q * UNIT, UNIT), UNIT)
        parts = pbuf[q * 4 + 3].astype(F32) + rdir[q, 0].astype(F32) + rdir[q, 1].astype(F32)
        grad = iv * (parts * ugain[:, at]) - xh[c, :, at].astype(F32) * coef
        og[q] = jnp.dot(tt[...], grad.astype(BF16), preferred_element_type=F32).astype(BF16)

        def send(d, carry):
            to = lax.rem(f + d, NF)
            here, there = og.at[q, ds(to, CAP)], inc.at[ds(f, CAP), pl.ds(q * UNIT, UNIT)]
            rcopy(here, there, b_s.at[q * NF + to], b_r.at[q * NF + f], fsdp=to)
            return carry

        lax.fori_loop(1, NF, send, 0)
        keep = pltpu.make_async_copy(
            og.at[q, ds(f, CAP)], inc.at[ds(f, CAP), pl.ds(q * UNIT, UNIT)], loc.at[10 + q]
        )
        keep.start()
        return keep

    back(0)
    back(1)
    far_out(0)
    back(2)
    arrived(sbuf.at[4], st_r.at[4])
    sbuf[x] = stat[rows_own, :] + sbuf[4]
    for n, to in enumerate((x1, x3, x2)):
        sends.append(rcopy(sbuf.at[x], sbuf.at[x], st_s.at[n], st_r.at[x], tensor=to))
    near_out(0)
    keep_a = pltpu.make_async_copy(attn.at[rows_own], attn_o.at[:, ds(c, HALF)], loc.at[12])
    keep_a.start()
    sends.append(rcopy(attn.at[rows_mate], attn_o.at[:, ds(c, HALF)], at_s, at_r, fsdp=mate))
    back(3)
    back(4)
    back(5)
    back(6)
    add_out(0)
    far_out(1)
    near_out(1)
    back(7)
    summed(3)
    summed(7)
    for frm in (x1, x3, x2):
        arrived(sbuf.at[frm], st_r.at[frm])
    add_out(1)
    keeps = [a_out(0)]
    keeps.append(a_out(1))

    def finish(d, carry):
        frm = lax.rem(f + d, NF)
        for q in range(2):
            block = inc.at[ds(frm, CAP), pl.ds(q * UNIT, UNIT)]
            arrived(block, b_r.at[q * NF + frm])
            arrived(og.at[q, ds(frm, CAP)], b_s.at[q * NF + frm])
        arrived(ids, id_s.at[frm])
        arrived(fnd.at[ds(frm, CAP)], a_s.at[frm])
        return carry

    lax.fori_loop(1, NF, finish, 0)
    arrived(attn_o.at[:, ds(1 - c, HALF)], at_r)
    for copy in keeps:
        copy.wait()
    keep_a.wait()
    for copy in sends:
        copy.wait_send()


ANY = pl.BlockSpec(memory_space=pl.ANY)
VMEM = pl.BlockSpec(memory_space=pltpu.VMEM)
DMA = pltpu.SemaphoreType.DMA


def layer(item_hidden, item_gain, wqkv, ids, grad_out, user_gain):
    vm = pltpu.VMEM
    return pl.pallas_call(
        layer_kernel,
        out_shape=(
            jax.ShapeDtypeStruct((ROWS, WIDTH), BF16),
            jax.ShapeDtypeStruct((SLOTS, ROWS), BF16),
            jax.ShapeDtypeStruct((ROWS, WIDTH), BF16),
            jax.ShapeDtypeStruct((SLOTS, WIDTH), BF16),
        ),
        in_specs=[ANY, VMEM, ANY, ANY, ANY, VMEM],
        out_specs=(VMEM, VMEM, ANY, ANY),
        scratch_shapes=[
            vm((ROWS * ITEM_LEN, WIDTH), BF16),
            vm((NF, 8, ROWS), jnp.int32),
            vm((NX, 128, 128), F32),
            vm((128, 128), F32),
            vm((SLOTS, ROWS), BF16),
            vm((SLOTS, WIDTH), BF16),
            vm((SLOTS, WIDTH), BF16),
            vm((ROWS, WIDTH), BF16),
            vm((D, ALL3), BF16),
            vm((2, ROWS, D), BF16),
            vm((BOTH, D), BF16),
            vm((2, BOTH, TRIO), F32),
            vm((BOTH, ALL3), BF16),
            vm((BOTH, ALL3), BF16),
            vm((2, ROWS, HALF), BF16),
            vm((BOTH, HALF), BF16),
            vm((BOTH, 128), F32),
            vm((BOTH, 128), F32),
            vm((5, ROWS, 128), F32),
            vm((8, BOTH, UNIT), BF16),
            vm((8, ROWS, UNIT), BF16),
            vm((8, ROWS, UNIT), BF16),
            vm((2, 2, ROWS, UNIT), BF16),
            vm((2, 2, ROWS // 2, UNIT), BF16),
            vm((2, SLOTS, UNIT), BF16),
            DMA((13,)),
            DMA((NF,)), DMA((NF,)),
            DMA((3,)), DMA((NX,)),
            DMA((NF,)), DMA((NF,)),
            DMA((64,)), DMA((2 * NF,)),
            DMA((6,)), DMA((6,)),
            DMA((6,)), DMA((2 * NX,)),
            DMA((4,)), DMA((NX,)),
            DMA, DMA,
            DMA, DMA,
            DMA((4,)), DMA((5,)),
            DMA((8,)), DMA((8,)),
            DMA((12,)), DMA((12,)),
            DMA((2 * NF,)), DMA((2 * NF,)),
        ],
        compiler_params=pltpu.CompilerParams(
            collective_id=0, has_side_effects=True, vmem_limit_bytes=62 * MIB
        ),
        cost_estimate=pl.CostEstimate(flops=27 * 10**9, bytes_accessed=64 * MIB, transcendentals=10**6),
        name="layer",
    )(item_hidden, item_gain, wqkv, ids, grad_out, user_gain)


def on_device(item_hidden, item_gain, occ_owner, occ_item, hist_len, user_gain, wqkv, grad_out):
    ids = jnp.stack(
        [occ_owner[:, 0], occ_item, jnp.broadcast_to(hist_len, (ROWS,))]
        + [jnp.zeros((ROWS,), jnp.int32)] * 5
    )
    item_embed, wanted, attended, incoming = layer(
        item_hidden, item_gain.reshape(1, WIDTH), wqkv, ids, grad_out, user_gain.reshape(1, D)
    )
    item_grads = lax.dot_general(
        wanted, incoming, (((0,), (0,)), ((), ())), preferred_element_type=F32
    )
    return (item_embed, attended, item_grads)


def solution(mesh):
    in_specs = (
        P("fsdp", "tensor"),
        P("tensor"),
        P("fsdp", None),
        P("fsdp"),
        P("fsdp"),
        P(),
        P(None, "fsdp", "tensor"),
        P("fsdp", "tensor"),
    )
    out_specs = (P("fsdp", "tensor"), P("fsdp", "tensor"), P("fsdp", "tensor"))
    return jax.shard_map(
        on_device, mesh=mesh, in_specs=in_specs, out_specs=out_specs, check_vma=False
    )
```

```python
import functools
import math

import jax
import jax.numpy as jnp
from jax import lax
from jax.experimental import pallas as pl
from jax.experimental.pallas import tpu as pltpu
from jax.sharding import PartitionSpec as P

D = 4096
HEAD_DIM = 128
ITEM_LEN = 8
EPSILON = 1e-05
NF = 32
NX = 4
ROWS = 256
CAP = 16
SLOTS = NF * CAP
WIDTH = D // NX
HALF = WIDTH // 2
SHARD = D // NF
GROUP = HALF // 2
TRIO = 3 * GROUP
PIECES = 4
UNIT = WIDTH // PIECES
PEERS = NF - 1
ALL3 = 2 * TRIO
BOTH = 2 * ROWS
F32 = jnp.float32
BF16 = jnp.bfloat16
MIB = 1 << 20


def rcopy(src, dst, send, recv, **where):
    copy = pltpu.make_async_remote_copy(
        src_ref=src,
        dst_ref=dst,
        send_sem=send,
        recv_sem=recv,
        device_id=where,
        device_id_type=pl.DeviceIdType.MESH,
    )
    copy.start()
    return copy


def arrived(ref, sem):
    pltpu.make_async_copy(ref, ref, sem).wait()


def greet():
    f, x = lax.axis_index("fsdp"), lax.axis_index("tensor")
    barrier = pltpu.get_barrier_semaphore()

    def signal(d, carry):
        pl.semaphore_signal(
            barrier,
            inc=1,
            device_id={"fsdp": lax.rem(f + d, NF)},
            device_id_type=pl.DeviceIdType.MESH,
        )
        return carry

    lax.fori_loop(1, NF, signal, 0)
    for d in range(1, NX):
        pl.semaphore_signal(
            barrier,
            inc=1,
            device_id={"tensor": lax.rem(x + d, NX)},
            device_id_type=pl.DeviceIdType.MESH,
        )


def greeted():
    pl.semaphore_wait(pltpu.get_barrier_semaphore(), NF - 1 + NX - 1)


def layer_kernel(
    hid, gain, w, ids, g, ugain,
    emb_o, oh_o, attn_o, inc,
    hid_v, idb, sqb, inv_v, tt, fnd, fet, share,
    wv, xh, nrm, acc, qkv, grads, gv, attn, inv_h, stat, sbuf, srow,
    dxs, cbuf, pbuf, rdir, rfwd, og,
    loc, id_s, id_r, sq_s, sq_r, a_s, a_r, w_s, w_r, wm_s, wm_r,
    x_s, x_r, p_s, p_r, g_s, g_r, at_s, at_r, st_s, st_r,
    c_s, c_r, r_s, r_r, b_s, b_r,
):
    f, x = lax.axis_index("fsdp"), lax.axis_index("tensor")
    c = lax.rem(f, 2)
    chip = f // 2
    z, y = lax.rem(chip, 4), chip // 4
    mate = f + 1 - 2 * c
    y1, y2, y3 = (lax.rem(y + d, 4) for d in (1, 2, 3))
    z1, z2, z3 = (lax.rem(z + d, 4) for d in (1, 2, 3))
    x1, x2, x3 = (lax.rem(x + d, 4) for d in (1, 2, 3))
    at_chip = lambda yy, zz: yy * 4 + zz
    yp, ym = at_chip(y1, z) * 2 + c, at_chip(y3, z) * 2 + c
    zp, zm = at_chip(y, z1) * 2 + c, at_chip(y, z3) * 2 + c
    sends = []

    def ds(i, n):
        return pl.ds(pl.multiple_of(i * n, n), n)

    load_hid = pltpu.make_async_copy(hid, hid_v, loc.at[0])
    load_hid.start()
    keep_w = []
    for h in range(2):
        for n in range(3):
            src = w.at[n, :, pl.ds(pl.multiple_of(c * HALF + h * GROUP, GROUP), GROUP)]
            dst = wv.at[ds(f, SHARD), pl.ds(h * TRIO + n * GROUP, GROUP)]
            keep_w.append(pltpu.make_async_copy(src, dst, loc.at[4 + h * 3 + n]))
            keep_w[-1].start()
    keep_id = pltpu.make_async_copy(ids, idb.at[f], loc.at[1])
    keep_id.start()
    keep_g = pltpu.make_async_copy(g.at[:, ds(c, HALF)], gv.at[c], loc.at[2])
    keep_g.start()
    greet()

    load_hid.wait()
    lane = lax.broadcasted_iota(jnp.int32, (128, 128), 1)

    def squares(k, total):
        v = hid_v[ds(k, 128), :].astype(F32)
        return jnp.where(lane == k, jnp.sum(v * v, axis=1, keepdims=True), total)

    sqb[x] = lax.fori_loop(0, 16, squares, jnp.zeros((128, 128), F32))
    greeted()

    def piece(h, s):
        return wv.at[ds(s, SHARD), pl.ds(h * TRIO, TRIO)]

    def part(h, s, k):
        at = pl.multiple_of(s * SHARD + k * (SHARD // 2), SHARD // 2)
        return wv.at[pl.ds(at, SHARD // 2), pl.ds(h * TRIO, TRIO)]

    wcount = [0]

    def wsend(ref, sem, dev):
        sends.append(rcopy(ref, ref, w_s.at[wcount[0]], w_r.at[sem], fsdp=dev))
        wcount[0] += 1

    def full(h, s, devs):
        for dev in devs:
            wsend(piece(h, s), (h * NF + s) * 2, dev)

    def half(h, s, k, dev):
        wsend(part(h, s, k), (h * NF + s) * 2 + k, dev)

    def got(h, s):
        arrived(piece(h, s), w_r.at[(h * NF + s) * 2])

    def got_halves(h, s):
        for k in range(2):
            arrived(part(h, s, k), w_r.at[(h * NF + s) * 2 + k])

    ways = ((yp, ym), (zp, zm))
    prev = (at_chip(y3, z) * 2, at_chip(y, z3) * 2 + 1)
    nxt = (at_chip(y1, z) * 2, at_chip(y, z1) * 2 + 1)
    far = (at_chip(y2, z) * 2, at_chip(y, z2) * 2 + 1)
    own = (chip * 2, chip * 2 + 1)

    for h in range(2):
        for n in range(3):
            src = w.at[n, :, pl.ds(pl.multiple_of((1 - c) * HALF + h * GROUP, GROUP), GROUP)]
            dst = wv.at[ds(f, SHARD), pl.ds(h * TRIO + n * GROUP, GROUP)]
            sends.append(rcopy(src, dst, wm_s.at[h * 3 + n], wm_r.at[h * 3 + n], fsdp=mate))
    first = (lax.select(c == 0, yp, zp), lax.select(c == 0, ym, zm))
    second = (lax.select(c == 0, zp, yp), lax.select(c == 0, zm, ym))
    for h in range(2):
        for copy in keep_w[3 * h : 3 * h + 3]:
            copy.wait()
        full(h, f, first)
        full(h, f, second)
    for n, to in enumerate((x1, x3, x2)):
        sends.append(rcopy(sqb.at[x], sqb.at[x], sq_s.at[n], sq_r.at[x], tensor=to))

    def id_send(d, carry):
        rcopy(ids, idb.at[f], id_s, id_r, fsdp=lax.rem(f + d, NF))
        return carry

    lax.fori_loop(1, NF, id_send, 0)
    sends.append(rcopy(g.at[:, ds(1 - c, HALF)], gv.at[c], g_s, g_r, fsdp=mate))

    for h in range(2):
        for n in range(3):
            dst = wv.at[ds(mate, SHARD), pl.ds(h * TRIO + n * GROUP, GROUP)]
            arrived(dst, wm_r.at[h * 3 + n])
        full(h, mate, second)
        full(h, mate, first)

    def second_near(h):
        for r in range(2):
            got(h, prev[r])
            half(h, prev[r], 0, ways[r][0])
            got(h, nxt[r])
            half(h, nxt[r], 1, ways[r][1])
        for r in range(2):
            full(h, prev[r], ways[1 - r])
            full(h, nxt[r], ways[1 - r])

    def second_far(h):
        for r in range(2):
            got_halves(h, far[r])
            full(h, far[r], ways[1 - r])

    def third(h, n):
        yy, zz = ((y, z), (y3, z3), (y1, z1), (y2, z2))[n]
        low = (at_chip(yy, z3) * 2, at_chip(y3, zz) * 2 + 1)
        high = (at_chip(yy, z1) * 2, at_chip(y1, zz) * 2 + 1)
        for r in range(2):
            got(h, low[r])
            half(h, low[r], 0, ways[1 - r][0])
            got(h, high[r])
            half(h, high[r], 1, ways[1 - r][1])

    def last(h, which):
        for n in which:
            yy, zz = ((y, z), (y3, z3), (y1, z1), (y2, z2))[n]
            got_halves(h, at_chip(yy, z2) * 2)
            got_halves(h, at_chip(y2, zz) * 2 + 1)

    arrived(idb.at[pl.ds(0, PEERS)], id_r)
    keep_id.wait()
    row = lax.broadcasted_iota(jnp.int32, (SLOTS, ROWS), 0)
    col = lax.broadcasted_iota(jnp.int32, (SLOTS, ROWS), 1)
    slot = lax.rem(row, CAP).astype(F32)
    group = row // CAP
    t_at = lax.broadcasted_iota(jnp.int32, (ROWS, ROWS), 0)
    s_at = lax.broadcasted_iota(jnp.int32, (ROWS, ROWS), 1)
    before = (t_at < s_at).astype(F32).astype(BF16)

    def slots_of(named):
        rank = jnp.dot(named.astype(F32).astype(BF16), before, preferred_element_type=F32)
        return named & (rank == slot)

    mine_owner = jnp.broadcast_to(idb[f, 0:1, :], (SLOTS, ROWS))
    tt[...] = slots_of(mine_owner == group).astype(F32).astype(BF16)
    table = idb[...].reshape(NF * 8, ROWS).astype(F32).astype(BF16)
    pick_owner = (col == group * 8).astype(F32).astype(BF16)
    pick_item = (col == group * 8 + 1).astype(F32).astype(BF16)
    owner_all = jnp.dot(pick_owner, table, preferred_element_type=F32)
    item_all = jnp.dot(pick_item, table, preferred_element_type=F32)
    taken = slots_of(owner_all == f.astype(F32))
    wanted = jnp.sum(jnp.where(taken, item_all + 1.0, 0.0), axis=1, keepdims=True) - 1.0
    oh_o[...] = (wanted == col.astype(F32)).astype(F32).astype(BF16)

    for frm in (x1, x3, x2):
        arrived(sqb.at[frm], sq_r.at[frm])
    inv_v[...] = lax.rsqrt((sqb[0] + sqb[1] + sqb[2] + sqb[3]) / D + EPSILON)

    def pool(k, carry):
        v = hid_v[ds(k, 128), :].astype(F32)
        inv = jnp.sum(jnp.where(lane == k, inv_v[...], 0.0), axis=1, keepdims=True)
        total = jnp.sum((v * inv).reshape(16, ITEM_LEN, WIDTH), axis=1)
        emb_o[ds(k, 16), :] = (total * (1.0 / ITEM_LEN) * gain[...]).astype(BF16)
        return carry

    lax.fori_loop(0, 16, pool, 0)
    fnd[...] = jnp.dot(oh_o[...], emb_o[...], preferred_element_type=F32).astype(BF16)

    def a_send(d, carry):
        to = lax.rem(f + d, NF)
        rcopy(fnd.at[ds(to, CAP)], fet.at[ds(f, CAP)], a_s, a_r, fsdp=to)
        return carry

    lax.fori_loop(1, NF, a_send, 0)
    fet[ds(f, CAP), :] = fnd[ds(f, CAP), :]
    second_near(0)
    third(0, 0)

    arrived(fet.at[pl.ds(0, PEERS * CAP)], a_r)
    share[...] = lax.dot_general(
        tt[...], fet[...], (((0,), (0,)), ((), ())), preferred_element_type=F32
    ).astype(BF16)

    def xpart(j, h):
        return xh.at[c, pl.ds(h * (ROWS // 2), ROWS // 2), ds(j, WIDTH)]

    def xwhole(k, j):
        return xh.at[k, :, ds(j, WIDTH)]

    keep_x = pltpu.make_async_copy(share, xwhole(c, x), loc.at[3])
    keep_x.start()
    for h in range(2):
        rows = share.at[pl.ds(h * (ROWS // 2), ROWS // 2)]
        sends.append(rcopy(rows, xpart(x, h), x_s.at[h], x_r.at[2 * x + h], tensor=x1))
        sends.append(rcopy(rows, xpart(x, h), x_s.at[2 + h], x_r.at[2 * x + h], tensor=x3))
    sends.append(rcopy(share, xwhole(c, x), p_s.at[0], p_r.at[x], fsdp=mate))

    def x_forward():
        for h, (frm, to) in enumerate(((x3, x1), (x1, x3))):
            arrived(xpart(frm, h), x_r.at[2 * frm + h])
            sends.append(rcopy(xpart(frm, h), xpart(frm, h), x_s.at[4 + h], x_r.at[2 * frm + h], tensor=to))
        for h, frm in enumerate((x3, x1)):
            arrived(xpart(frm, 1 - h), x_r.at[2 * frm + 1 - h])
            sends.append(rcopy(xwhole(c, frm), xwhole(c, frm), p_s.at[1 + h], p_r.at[frm], fsdp=mate))

    def x_finish():
        for h in range(2):
            arrived(xpart(x2, h), x_r.at[2 * x2 + h])
        sends.append(rcopy(xwhole(c, x2), xwhole(c, x2), p_s.at[3], p_r.at[x2], fsdp=mate))
        keep_x.wait()

    def norm(k, carry):
        h, m = k // 8, lax.rem(k, 8)
        v = xh[h, ds(m, 32), :].astype(F32)
        inv = lax.rsqrt(jnp.sum(v * v, axis=1, keepdims=True) / D + EPSILON)
        nrm[ds(k, 32), :] = (v * inv * ugain[...]).astype(BF16)
        inv_h[ds(k, 32), :] = jnp.broadcast_to(inv, (32, 128))
        return carry

    def project(h, k, depth):
        acc[h] += jnp.dot(
            nrm[:, ds(k, depth)],
            wv[ds(k, depth), h * TRIO : (h + 1) * TRIO],
            preferred_element_type=F32,
        )

    def project_near(h):
        def block(t, carry):
            yy, zz = lax.rem(y + 3 + t // 3, 4), lax.rem(z + 3 + lax.rem(t, 3), 4)
            project(h, at_chip(yy, zz), 256)
            return carry

        lax.fori_loop(0, 9, block, 0)

    def project_far(h):
        def block(t, carry):
            yy, zz = lax.rem(y + 3 + t, 4), lax.rem(z + 3 + t, 4)
            project(h, at_chip(yy, z2), 256)
            project(h, at_chip(y2, zz), 256)
            return carry

        lax.fori_loop(0, 3, block, 0)

    def project_last(h):
        project(h, at_chip(y2, z2), 256)
        qkv[:, h * TRIO : (h + 1) * TRIO] = acc[h].astype(BF16)

    acc[...] = jnp.zeros_like(acc)
    second_far(0)
    third(0, 1)
    third(0, 2)
    x_forward()
    third(0, 3)
    second_near(1)
    third(1, 0)
    x_finish()
    lax.fori_loop(c * 8, c * 8 + 8, norm, 0)
    second_far(1)
    for j in (x, x3, x1, x2):
        arrived(xwhole(1 - c, j), p_r.at[j])
    lax.fori_loop((1 - c) * 8, (1 - c) * 8 + 8, norm, 0)
    project_near(0)
    third(1, 1)
    last(0, (0, 1, 2, 3))
    project_far(0)
    project_last(0)
    third(1, 2)

    factor = 1.0 / math.sqrt(HEAD_DIM)
    t_row = lax.broadcasted_iota(jnp.int32, (ROWS, HEAD_DIM), 0)
    nt = (((1,), (1,)), ((), ()))
    tn = (((0,), (0,)), ((), ()))
    keep_g.wait()
    arrived(gv.at[1 - c], g_r)

    def attend(k, carry):
        h, n = lax.rem(k, 2), k // 2
        rows = ds(h, ROWS)
        cols = ds(n, HEAD_DIM)
        base = (n // 2) * TRIO + lax.rem(n, 2) * HEAD_DIM
        q_at, k_at, v_at = (
            pl.ds(pl.multiple_of(base + i * GROUP, HEAD_DIM), HEAD_DIM) for i in range(3)
        )
        length = idb[chip * 2 + h, 2:3, :]
        allowed = (s_at <= t_at) & (s_at < length)
        live = t_row < length[:, :HEAD_DIM]
        qq, kk, vv = qkv[rows, q_at], qkv[rows, k_at], qkv[rows, v_at]
        gg = jnp.where(live, gv[h, :, cols].astype(F32), 0.0).astype(BF16)
        scores = lax.dot_general(qq, kk, nt, preferred_element_type=F32) * factor
        scores = jnp.where(allowed, scores, -1e30)
        top = jnp.max(scores, axis=1, keepdims=True)
        raised = jnp.where(allowed, jnp.exp(scores - top), 0.0)
        probs = raised * (1.0 / jnp.sum(raised, axis=1, keepdims=True))
        pb = probs.astype(BF16)
        out = jnp.dot(pb, vv, preferred_element_type=F32)
        out = jnp.where(live, out, 0.0).astype(BF16)
        cols_o = pl.ds(pl.multiple_of(c * HALF + n * HEAD_DIM, HEAD_DIM), HEAD_DIM)

        @pl.when(h == c)
        def _():
            attn_o[:, cols_o] = out

        @pl.when(h != c)
        def _():
            attn[:, cols] = out

        dv = lax.dot_general(pb, gg, tn, preferred_element_type=F32).astype(BF16)
        dp = lax.dot_general(gg, vv, nt, preferred_element_type=F32)
        mid = jnp.sum(probs * dp, axis=1, keepdims=True)
        dsc = (probs * (dp - mid) * factor).astype(BF16)
        dq = jnp.dot(dsc, kk, preferred_element_type=F32).astype(BF16)
        dk = lax.dot_general(dsc, qq, tn, preferred_element_type=F32).astype(BF16)
        grads[rows, q_at] = dq
        grads[rows, k_at] = dk
        grads[rows, v_at] = dv
        terms = (
            dq.astype(F32) * qq.astype(F32)
            + dk.astype(F32) * kk.astype(F32)
            + dv.astype(F32) * vv.astype(F32)
        )
        stat[rows, :] += jnp.broadcast_to(jnp.sum(terms, axis=1, keepdims=True), (ROWS, 128))
        return carry

    stat[...] = jnp.zeros_like(stat)
    lax.fori_loop(0, 4, attend, 0)
    third(1, 3)
    project_near(1)
    last(1, (0, 1, 2))
    project_far(1)
    last(1, (3,))
    project_last(1)
    lax.fori_loop(4, 8, attend, 0)

    rows_own, rows_mate = ds(c, ROWS), ds(1 - c, ROWS)
    low, high = pl.ds(0, ROWS // 2), pl.ds(ROWS // 2, ROWS // 2)
    sends.append(rcopy(stat.at[rows_mate], sbuf, st_s.at[3], st_r.at[4], fsdp=mate))
    order = (x2, x1, x3, x)

    def back(q, n):
        u = q * 4 + n
        at = pl.ds(pl.multiple_of(order[n] * WIDTH + q * UNIT, UNIT), UNIT)
        dxs[u] = lax.dot_general(grads[...], wv[at, :], nt, preferred_element_type=F32).astype(BF16)
        sends.append(rcopy(dxs.at[u, rows_mate], cbuf.at[u], c_s.at[u], c_r.at[u], fsdp=mate))

    def summed(u):
        arrived(cbuf.at[u], c_r.at[u])
        pbuf[u] = (dxs[u, rows_own, :].astype(F32) + cbuf[u].astype(F32)).astype(BF16)

    def ring(q, k, src, dst, to):
        sends.append(rcopy(src, dst, r_s.at[q * 6 + k], r_r.at[q * 6 + k], tensor=to))

    def far_out(q):
        summed(q * 4)
        ring(q, 0, pbuf.at[q * 4, low], rfwd.at[q, 0], x1)
        ring(q, 1, pbuf.at[q * 4, high], rfwd.at[q, 1], x3)

    def near_out(q):
        summed(q * 4 + 1)
        ring(q, 2, pbuf.at[q * 4 + 1, high], rdir.at[q, 0, high], x1)
        summed(q * 4 + 2)
        ring(q, 3, pbuf.at[q * 4 + 2, low], rdir.at[q, 1, low], x3)

    def add_out(q):
        for k, rows, to in ((0, low, x1), (1, high, x3)):
            u = q * 4 + 1 + k
            arrived(rfwd.at[q, k], r_r.at[q * 6 + k])
            pbuf[u, rows, :] = (pbuf[u, rows, :].astype(F32) + rfwd[q, k].astype(F32)).astype(BF16)
            ring(q, 4 + k, pbuf.at[u, rows], rdir.at[q, k, rows], to)

    def a_out(q):
        for k, rows in ((0, high), (1, low)):
            arrived(rdir.at[q, k, rows], r_r.at[q * 6 + 2 + k])
        for k, rows in ((0, low), (1, high)):
            arrived(rdir.at[q, k, rows], r_r.at[q * 6 + 4 + k])
        at = pl.ds(pl.multiple_of(x * WIDTH + q * UNIT, UNIT), UNIT)
        parts = pbuf[q * 4 + 3].astype(F32) + rdir[q, 0].astype(F32) + rdir[q, 1].astype(F32)
        grad = iv * (parts * ugain[:, at]) - xh[c, :, at].astype(F32) * coef
        og[q] = jnp.dot(tt[...], grad.astype(BF16), preferred_element_type=F32).astype(BF16)

        def send(d, carry):
            to = lax.rem(f + d, NF)
            here, there = og.at[q, ds(to, CAP)], inc.at[ds(f, CAP), pl.ds(q * UNIT, UNIT)]
            rcopy(here, there, b_s.at[q], b_r.at[q], fsdp=to)
            return carry

        lax.fori_loop(1, NF, send, 0)
        keep = pltpu.make_async_copy(
            og.at[q, ds(f, CAP)], inc.at[ds(f, CAP), pl.ds(q * UNIT, UNIT)], loc.at[10 + q]
        )
        keep.start()
        return keep

    def stat_out():
        arrived(sbuf, st_r.at[4])
        both = stat[rows_own, :] + sbuf[...]
        srow[x] = jnp.transpose(both)[0:8, :]
        for n, to in enumerate((x1, x3, x2)):
            sends.append(rcopy(srow.at[x], srow.at[x], st_s.at[n], st_r.at[x], tensor=to))

    def stat_in():
        for frm in (x1, x3, x2):
            arrived(srow.at[frm], st_r.at[frm])
        total = (srow[0] + srow[1] + srow[2] + srow[3])[0:1, :]
        full_rows = jnp.transpose(jnp.broadcast_to(total, (128, ROWS)))
        iv = inv_h[rows_own, 0:1]
        coef = iv * iv * full_rows[:, 0:1] / D
        return iv, coef

    for q, n in ((0, 0), (0, 1), (0, 2), (1, 0)):
        back(q, n)
    far_out(0)
    back(1, 1)
    near_out(0)
    back(1, 2)
    far_out(1)
    stat_out()
    back(2, 0)
    back(2, 1)
    add_out(0)
    near_out(1)
    back(2, 2)
    back(0, 3)
    far_out(2)
    back(3, 0)
    back(1, 3)
    add_out(1)
    near_out(2)
    back(3, 1)
    back(3, 2)
    far_out(3)
    summed(3)
    iv, coef = stat_in()
    keeps = [a_out(0)]
    back(2, 3)
    back(3, 3)
    add_out(2)
    near_out(3)
    sends.append(rcopy(attn, attn_o.at[:, ds(c, HALF)], at_s, at_r, fsdp=mate))
    summed(7)
    keeps.append(a_out(1))
    add_out(3)
    summed(11)
    keeps.append(a_out(2))
    summed(15)
    keeps.append(a_out(3))

    for q in range(PIECES):
        arrived(inc.at[pl.ds(0, PEERS * CAP), pl.ds(q * UNIT, UNIT)], b_r.at[q])
        arrived(og.at[q, pl.ds(0, PEERS * CAP)], b_s.at[q])
    arrived(idb.at[pl.ds(0, PEERS)], id_s)
    arrived(fnd.at[pl.ds(0, PEERS * CAP)], a_s)
    arrived(attn_o.at[:, ds(1 - c, HALF)], at_r)
    for copy in keeps:
        copy.wait()
    for copy in sends:
        copy.wait_send()


ANY = pl.BlockSpec(memory_space=pl.ANY)
VMEM = pl.BlockSpec(memory_space=pltpu.VMEM)
DMA = pltpu.SemaphoreType.DMA


def layer(item_hidden, item_gain, wqkv, ids, grad_out, user_gain):
    vm = pltpu.VMEM
    return pl.pallas_call(
        layer_kernel,
        out_shape=(
            jax.ShapeDtypeStruct((ROWS, WIDTH), BF16),
            jax.ShapeDtypeStruct((SLOTS, ROWS), BF16),
            jax.ShapeDtypeStruct((ROWS, WIDTH), BF16),
            jax.ShapeDtypeStruct((SLOTS, WIDTH), BF16),
        ),
        in_specs=[ANY, VMEM, ANY, ANY, ANY, VMEM],
        out_specs=(VMEM, VMEM, VMEM, ANY),
        scratch_shapes=[
            vm((ROWS * ITEM_LEN, WIDTH), BF16),
            vm((NF, 8, ROWS), jnp.int32),
            vm((NX, 128, 128), F32),
            vm((128, 128), F32),
            vm((SLOTS, ROWS), BF16),
            vm((SLOTS, WIDTH), BF16),
            vm((SLOTS, WIDTH), BF16),
            vm((ROWS, WIDTH), BF16),
            vm((D, ALL3), BF16),
            vm((2, ROWS, D), BF16),
            vm((BOTH, D), BF16),
            vm((2, BOTH, TRIO), F32),
            vm((BOTH, ALL3), BF16),
            vm((BOTH, ALL3), BF16),
            vm((2, ROWS, HALF), BF16),
            vm((ROWS, HALF), BF16),
            vm((BOTH, 128), F32),
            vm((BOTH, 128), F32),
            vm((ROWS, 128), F32),
            vm((NX, 8, ROWS), F32),
            vm((4 * PIECES, BOTH, UNIT), BF16),
            vm((4 * PIECES, ROWS, UNIT), BF16),
            vm((4 * PIECES, ROWS, UNIT), BF16),
            vm((PIECES, 2, ROWS, UNIT), BF16),
            vm((PIECES, 2, ROWS // 2, UNIT), BF16),
            vm((PIECES, SLOTS, UNIT), BF16),
            DMA((10 + PIECES,)),
            DMA, DMA,
            DMA((3,)), DMA((NX,)),
            DMA, DMA,
            DMA((80,)), DMA((4 * NF,)),
            DMA((6,)), DMA((6,)),
            DMA((6,)), DMA((2 * NX,)),
            DMA((4,)), DMA((NX,)),
            DMA, DMA,
            DMA, DMA,
            DMA((4,)), DMA((5,)),
            DMA((4 * PIECES,)), DMA((4 * PIECES,)),
            DMA((6 * PIECES,)), DMA((6 * PIECES,)),
            DMA((PIECES,)), DMA((PIECES,)),
        ],
        compiler_params=pltpu.CompilerParams(
            collective_id=0, has_side_effects=True, vmem_limit_bytes=62 * MIB
        ),
        cost_estimate=pl.CostEstimate(flops=27 * 10**9, bytes_accessed=64 * MIB, transcendentals=10**6),
        name="layer",
    )(item_hidden, item_gain, wqkv, ids, grad_out, user_gain)


def closing_kernel(emb, attn, oh, inc, emb_o, attn_o, grads_o, oh_v, inc_v, emb_v, attn_v, sem):
    pairs = ((oh, oh_v), (inc, inc_v), (emb, emb_v), (attn, attn_v), (emb_v, emb_o), (attn_v, attn_o))
    copies = [pltpu.make_async_copy(src, dst, sem.at[n]) for n, (src, dst) in enumerate(pairs)]
    for copy in copies[:4]:
        copy.start()
    for n in (2, 3):
        copies[n].wait()
        copies[n + 2].start()
    for copy in copies[:2]:
        copy.wait()
    grads_o[...] = lax.dot_general(
        oh_v[...], inc_v[...], (((0,), (0,)), ((), ())), preferred_element_type=F32
    )
    for copy in copies[4:]:
        copy.wait()


def closing(item_embed, attended, wanted, incoming):
    return pl.pallas_call(
        closing_kernel,
        out_shape=(
            jax.ShapeDtypeStruct((ROWS, WIDTH), BF16),
            jax.ShapeDtypeStruct((ROWS, WIDTH), BF16),
            jax.ShapeDtypeStruct((ROWS, WIDTH), F32),
        ),
        in_specs=[ANY] * 4,
        out_specs=(ANY, ANY, VMEM),
        scratch_shapes=[
            pltpu.VMEM((SLOTS, ROWS), BF16),
            pltpu.VMEM((SLOTS, WIDTH), BF16),
            pltpu.VMEM((ROWS, WIDTH), BF16),
            pltpu.VMEM((ROWS, WIDTH), BF16),
            DMA((6,)),
        ],
        compiler_params=pltpu.CompilerParams(vmem_limit_bytes=62 * MIB),
        cost_estimate=pl.CostEstimate(flops=3 * 10**8, bytes_accessed=5 * MIB, transcendentals=0),
        name="closing",
    )(item_embed, attended, wanted, incoming)


def on_device(item_hidden, item_gain, occ_owner, occ_item, hist_len, user_gain, wqkv, grad_out):
    ids = jnp.stack(
        [occ_owner[:, 0], occ_item, jnp.broadcast_to(hist_len, (ROWS,))]
        + [jnp.zeros((ROWS,), jnp.int32)] * 5
    )
    item_embed, wanted, attended, incoming = layer(
        item_hidden, item_gain.reshape(1, WIDTH), wqkv, ids, grad_out, user_gain.reshape(1, D)
    )
    return closing(item_embed, attended, wanted, incoming)


def solution(mesh):
    in_specs = (
        P("fsdp", "tensor"),
        P("tensor"),
        P("fsdp", None),
        P("fsdp"),
        P("fsdp"),
        P(),
        P(None, "fsdp", "tensor"),
        P("fsdp", "tensor"),
    )
    out_specs = (P("fsdp", "tensor"), P("fsdp", "tensor"), P("fsdp", "tensor"))
    return jax.shard_map(
        on_device, mesh=mesh, in_specs=in_specs, out_specs=out_specs, check_vma=False
    )
```

```python
import functools
import math

import jax
import jax.numpy as jnp
from jax import lax
from jax.experimental import pallas as pl
from jax.experimental.pallas import tpu as pltpu
from jax.sharding import PartitionSpec as P

D = 4096
HEAD_DIM = 128
ITEM_LEN = 8
EPSILON = 1e-05
NF = 32
NX = 4
ROWS = 256
CAP = 16
SLOTS = NF * CAP
WIDTH = D // NX
HALF = WIDTH // 2
SHARD = D // NF
GROUP = HALF // 2
TRIO = 3 * GROUP
PIECES = 4
UNIT = WIDTH // PIECES
PEERS = NF - 1
ALL3 = 2 * TRIO
BOTH = 2 * ROWS
F32 = jnp.float32
BF16 = jnp.bfloat16
MIB = 1 << 20


def rcopy(src, dst, send, recv, **where):
    copy = pltpu.make_async_remote_copy(
        src_ref=src,
        dst_ref=dst,
        send_sem=send,
        recv_sem=recv,
        device_id=where,
        device_id_type=pl.DeviceIdType.MESH,
    )
    copy.start()
    return copy


def arrived(ref, sem):
    pltpu.make_async_copy(ref, ref, sem).wait()


def greet():
    f, x = lax.axis_index("fsdp"), lax.axis_index("tensor")
    barrier = pltpu.get_barrier_semaphore()

    def signal(d, carry):
        pl.semaphore_signal(
            barrier,
            inc=1,
            device_id={"fsdp": lax.rem(f + d, NF)},
            device_id_type=pl.DeviceIdType.MESH,
        )
        return carry

    lax.fori_loop(1, NF, signal, 0)
    for d in range(1, NX):
        pl.semaphore_signal(
            barrier,
            inc=1,
            device_id={"tensor": lax.rem(x + d, NX)},
            device_id_type=pl.DeviceIdType.MESH,
        )


def greeted():
    pl.semaphore_wait(pltpu.get_barrier_semaphore(), NF - 1 + NX - 1)


def layer_kernel(
    hid, gain, w, ids, g, ugain,
    emb_o, oh_o, attn_o, inc,
    hid_v, idb, sqb, inv_v, tt, fnd, fet, share,
    wv, xh, nrm, acc, qkv, grads, gv, attn, inv_h, stat, sbuf, srow,
    dx0, dxs, cbuf, pbuf, rdir, rfwd, og,
    loc, id_s, id_r, sq_s, sq_r, a_s, a_r, w_s, w_r, wm_s, wm_r,
    x_s, x_r, p_s, p_r, g_s, g_r, at_s, at_r, st_s, st_r,
    c_s, c_r, r_s, r_r, b_s, b_r,
):
    f, x = lax.axis_index("fsdp"), lax.axis_index("tensor")
    c = lax.rem(f, 2)
    chip = f // 2
    z, y = lax.rem(chip, 4), chip // 4
    mate = f + 1 - 2 * c
    y1, y2, y3 = (lax.rem(y + d, 4) for d in (1, 2, 3))
    z1, z2, z3 = (lax.rem(z + d, 4) for d in (1, 2, 3))
    x1, x2, x3 = (lax.rem(x + d, 4) for d in (1, 2, 3))
    at_chip = lambda yy, zz: yy * 4 + zz
    yp, ym = at_chip(y1, z) * 2 + c, at_chip(y3, z) * 2 + c
    zp, zm = at_chip(y, z1) * 2 + c, at_chip(y, z3) * 2 + c
    sends = []

    def ds(i, n):
        return pl.ds(pl.multiple_of(i * n, n), n)

    load_hid = pltpu.make_async_copy(hid, hid_v, loc.at[0])
    load_hid.start()
    keep_w = []
    for h in range(2):
        for n in range(3):
            src = w.at[n, :, pl.ds(pl.multiple_of(c * HALF + h * GROUP, GROUP), GROUP)]
            dst = wv.at[ds(f, SHARD), pl.ds(h * TRIO + n * GROUP, GROUP)]
            keep_w.append(pltpu.make_async_copy(src, dst, loc.at[4 + h * 3 + n]))
            keep_w[-1].start()
    keep_id = pltpu.make_async_copy(ids, idb.at[f], loc.at[1])
    keep_id.start()
    keep_g = pltpu.make_async_copy(g.at[:, ds(c, HALF)], gv.at[c], loc.at[2])
    keep_g.start()
    greet()

    lane = lax.broadcasted_iota(jnp.int32, (128, 128), 1)

    def squares(k, total):
        v = hid_v[ds(k, 128), :].astype(F32)
        return jnp.where(lane == k, jnp.sum(v * v, axis=1, keepdims=True), total)

    greeted()

    def piece(h, s):
        return wv.at[ds(s, SHARD), pl.ds(h * TRIO, TRIO)]

    def part(h, s, k):
        at = pl.multiple_of(s * SHARD + k * (SHARD // 2), SHARD // 2)
        return wv.at[pl.ds(at, SHARD // 2), pl.ds(h * TRIO, TRIO)]

    wcount = [0]

    def wsend(ref, sem, dev):
        sends.append(rcopy(ref, ref, w_s.at[wcount[0]], w_r.at[sem], fsdp=dev))
        wcount[0] += 1

    def full(h, s, devs):
        for dev in devs:
            wsend(piece(h, s), (h * NF + s) * 2, dev)

    def half(h, s, k, dev):
        wsend(part(h, s, k), (h * NF + s) * 2 + k, dev)

    def got(h, s):
        arrived(piece(h, s), w_r.at[(h * NF + s) * 2])

    def got_halves(h, s):
        for k in range(2):
            arrived(part(h, s, k), w_r.at[(h * NF + s) * 2 + k])

    ways = ((yp, ym), (zp, zm))
    prev = (at_chip(y3, z) * 2, at_chip(y, z3) * 2 + 1)
    nxt = (at_chip(y1, z) * 2, at_chip(y, z1) * 2 + 1)
    far = (at_chip(y2, z) * 2, at_chip(y, z2) * 2 + 1)
    own = (chip * 2, chip * 2 + 1)

    for h in range(2):
        for n in range(3):
            src = w.at[n, :, pl.ds(pl.multiple_of((1 - c) * HALF + h * GROUP, GROUP), GROUP)]
            dst = wv.at[ds(f, SHARD), pl.ds(h * TRIO + n * GROUP, GROUP)]
            sends.append(rcopy(src, dst, wm_s.at[h * 3 + n], wm_r.at[h * 3 + n], fsdp=mate))
    first = (lax.select(c == 0, yp, zp), lax.select(c == 0, ym, zm))
    second = (lax.select(c == 0, zp, yp), lax.select(c == 0, zm, ym))
    for h in range(2):
        for copy in keep_w[3 * h : 3 * h + 3]:
            copy.wait()
        full(h, f, first)
        full(h, f, second)
    load_hid.wait()
    sqb[x] = lax.fori_loop(0, 16, squares, jnp.zeros((128, 128), F32))
    for n, to in enumerate((x1, x3, x2)):
        sends.append(rcopy(sqb.at[x], sqb.at[x], sq_s.at[n], sq_r.at[x], tensor=to))

    def id_send(d, carry):
        rcopy(ids, idb.at[f], id_s, id_r, fsdp=lax.rem(f + d, NF))
        return carry

    lax.fori_loop(1, NF, id_send, 0)
    sends.append(rcopy(g.at[:, ds(1 - c, HALF)], gv.at[c], g_s, g_r, fsdp=mate))

    for h in range(2):
        for n in range(3):
            dst = wv.at[ds(mate, SHARD), pl.ds(h * TRIO + n * GROUP, GROUP)]
            arrived(dst, wm_r.at[h * 3 + n])
        full(h, mate, second)
        full(h, mate, first)

    def second_near(h):
        for r in range(2):
            got(h, prev[r])
            half(h, prev[r], 0, ways[r][0])
            got(h, nxt[r])
            half(h, nxt[r], 1, ways[r][1])
        for r in range(2):
            full(h, prev[r], ways[1 - r])
            full(h, nxt[r], ways[1 - r])

    def second_far(h):
        for r in range(2):
            got_halves(h, far[r])
            full(h, far[r], ways[1 - r])

    def third(h, n):
        yy, zz = ((y, z), (y3, z3), (y1, z1), (y2, z2))[n]
        low = (at_chip(yy, z3) * 2, at_chip(y3, zz) * 2 + 1)
        high = (at_chip(yy, z1) * 2, at_chip(y1, zz) * 2 + 1)
        for r in range(2):
            got(h, low[r])
            half(h, low[r], 0, ways[1 - r][0])
            got(h, high[r])
            half(h, high[r], 1, ways[1 - r][1])

    def last(h, which):
        for n in which:
            yy, zz = ((y, z), (y3, z3), (y1, z1), (y2, z2))[n]
            got_halves(h, at_chip(yy, z2) * 2)
            got_halves(h, at_chip(y2, zz) * 2 + 1)

    arrived(idb.at[pl.ds(0, PEERS)], id_r)
    keep_id.wait()
    row = lax.broadcasted_iota(jnp.int32, (SLOTS, ROWS), 0)
    col = lax.broadcasted_iota(jnp.int32, (SLOTS, ROWS), 1)
    slot = lax.rem(row, CAP).astype(F32)
    group = row // CAP
    t_at = lax.broadcasted_iota(jnp.int32, (ROWS, ROWS), 0)
    s_at = lax.broadcasted_iota(jnp.int32, (ROWS, ROWS), 1)
    before = (t_at < s_at).astype(F32).astype(BF16)

    def slots_of(named):
        rank = jnp.dot(named.astype(F32).astype(BF16), before, preferred_element_type=F32)
        return named & (rank == slot)

    mine_owner = jnp.broadcast_to(idb[f, 0:1, :], (SLOTS, ROWS))
    tt[...] = slots_of(mine_owner == group).astype(F32).astype(BF16)
    table = idb[...].reshape(NF * 8, ROWS).astype(F32).astype(BF16)
    pick_owner = (col == group * 8).astype(F32).astype(BF16)
    pick_item = (col == group * 8 + 1).astype(F32).astype(BF16)
    owner_all = jnp.dot(pick_owner, table, preferred_element_type=F32)
    item_all = jnp.dot(pick_item, table, preferred_element_type=F32)
    taken = slots_of(owner_all == f.astype(F32))
    wanted = jnp.sum(jnp.where(taken, item_all + 1.0, 0.0), axis=1, keepdims=True) - 1.0
    oh_o[...] = (wanted == col.astype(F32)).astype(F32).astype(BF16)

    for frm in (x1, x3, x2):
        arrived(sqb.at[frm], sq_r.at[frm])
    inv_v[...] = lax.rsqrt((sqb[0] + sqb[1] + sqb[2] + sqb[3]) / D + EPSILON)

    def pool(k, carry):
        v = hid_v[ds(k, 128), :].astype(F32)
        inv = jnp.sum(jnp.where(lane == k, inv_v[...], 0.0), axis=1, keepdims=True)
        total = jnp.sum((v * inv).reshape(16, ITEM_LEN, WIDTH), axis=1)
        emb_o[ds(k, 16), :] = (total * (1.0 / ITEM_LEN) * gain[...]).astype(BF16)
        return carry

    lax.fori_loop(0, 16, pool, 0)
    fnd[...] = jnp.dot(oh_o[...], emb_o[...], preferred_element_type=F32).astype(BF16)

    def a_send(d, carry):
        to = lax.rem(f + d, NF)
        rcopy(fnd.at[ds(to, CAP)], fet.at[ds(f, CAP)], a_s, a_r, fsdp=to)
        return carry

    lax.fori_loop(1, NF, a_send, 0)
    fet[ds(f, CAP), :] = fnd[ds(f, CAP), :]
    second_near(0)
    third(0, 0)

    arrived(fet.at[pl.ds(0, PEERS * CAP)], a_r)
    share[...] = lax.dot_general(
        tt[...], fet[...], (((0,), (0,)), ((), ())), preferred_element_type=F32
    ).astype(BF16)

    def xpart(j, h):
        return xh.at[c, pl.ds(h * (ROWS // 2), ROWS // 2), ds(j, WIDTH)]

    def xwhole(k, j):
        return xh.at[k, :, ds(j, WIDTH)]

    keep_x = pltpu.make_async_copy(share, xwhole(c, x), loc.at[3])
    keep_x.start()
    for h in range(2):
        rows = share.at[pl.ds(h * (ROWS // 2), ROWS // 2)]
        sends.append(rcopy(rows, xpart(x, h), x_s.at[h], x_r.at[2 * x + h], tensor=x1))
        sends.append(rcopy(rows, xpart(x, h), x_s.at[2 + h], x_r.at[2 * x + h], tensor=x3))
    sends.append(rcopy(share, xwhole(c, x), p_s.at[0], p_r.at[x], fsdp=mate))

    def x_forward():
        for h, (frm, to) in enumerate(((x3, x1), (x1, x3))):
            arrived(xpart(frm, h), x_r.at[2 * frm + h])
            sends.append(rcopy(xpart(frm, h), xpart(frm, h), x_s.at[4 + h], x_r.at[2 * frm + h], tensor=to))
        for h, frm in enumerate((x3, x1)):
            arrived(xpart(frm, 1 - h), x_r.at[2 * frm + 1 - h])
            sends.append(rcopy(xwhole(c, frm), xwhole(c, frm), p_s.at[1 + h], p_r.at[frm], fsdp=mate))

    def x_finish():
        for h in range(2):
            arrived(xpart(x2, h), x_r.at[2 * x2 + h])
        sends.append(rcopy(xwhole(c, x2), xwhole(c, x2), p_s.at[3], p_r.at[x2], fsdp=mate))
        keep_x.wait()

    def norm(k, carry):
        h, m = k // 8, lax.rem(k, 8)
        v = xh[h, ds(m, 32), :].astype(F32)
        inv = lax.rsqrt(jnp.sum(v * v, axis=1, keepdims=True) / D + EPSILON)
        nrm[ds(k, 32), :] = (v * inv * ugain[...]).astype(BF16)
        inv_h[ds(k, 32), :] = jnp.broadcast_to(inv, (32, 128))
        return carry

    def project(k):
        acc[...] += jnp.dot(
            nrm[:, ds(k, 256)], wv[ds(k, 256), TRIO:ALL3], preferred_element_type=F32
        )

    def project_near():
        def block(t, carry):
            yy, zz = lax.rem(y + 3 + t // 3, 4), lax.rem(z + 3 + lax.rem(t, 3), 4)
            project(at_chip(yy, zz))
            return carry

        lax.fori_loop(0, 9, block, 0)

    def project_far():
        def block(t, carry):
            yy, zz = lax.rem(y + 3 + t, 4), lax.rem(z + 3 + t, 4)
            project(at_chip(yy, z2))
            project(at_chip(y2, zz))
            return carry

        lax.fori_loop(0, 3, block, 0)

    def project_last():
        project(at_chip(y2, z2))
        qkv[:, TRIO:ALL3] = acc[...].astype(BF16)

    acc[...] = jnp.zeros_like(acc)
    second_far(0)
    third(0, 1)
    third(0, 2)
    x_forward()
    third(0, 3)
    second_near(1)
    third(1, 0)
    x_finish()
    lax.fori_loop(c * 8, c * 8 + 8, norm, 0)
    second_far(1)
    for j in (x, x3, x1, x2):
        arrived(xwhole(1 - c, j), p_r.at[j])
    lax.fori_loop((1 - c) * 8, (1 - c) * 8 + 8, norm, 0)
    last(0, (0, 1, 2, 3))

    def project_all(n, carry):
        at = ds(n, GROUP)
        qkv[:, at] = jnp.dot(nrm[...], wv[:, at], preferred_element_type=F32).astype(BF16)
        return carry

    lax.fori_loop(0, 3, project_all, 0)
    third(1, 1)

    factor = 1.0 / math.sqrt(HEAD_DIM)
    t_row = lax.broadcasted_iota(jnp.int32, (ROWS, HEAD_DIM), 0)
    nt = (((1,), (1,)), ((), ()))
    tn = (((0,), (0,)), ((), ()))
    keep_g.wait()
    arrived(gv.at[1 - c], g_r)

    def attend(k, carry):
        h, n = lax.rem(k, 2), k // 2
        rows = ds(h, ROWS)
        cols = ds(n, HEAD_DIM)
        base = (n // 2) * TRIO + lax.rem(n, 2) * HEAD_DIM
        q_at, k_at, v_at = (
            pl.ds(pl.multiple_of(base + i * GROUP, HEAD_DIM), HEAD_DIM) for i in range(3)
        )
        length = idb[chip * 2 + h, 2:3, :]
        allowed = (s_at <= t_at) & (s_at < length)
        live = t_row < length[:, :HEAD_DIM]
        qq, kk, vv = qkv[rows, q_at], qkv[rows, k_at], qkv[rows, v_at]
        gg = jnp.where(live, gv[h, :, cols].astype(F32), 0.0).astype(BF16)
        scores = lax.dot_general(qq, kk, nt, preferred_element_type=F32) * factor
        scores = jnp.where(allowed, scores, -1e30)
        top = jnp.max(scores, axis=1, keepdims=True)
        raised = jnp.where(allowed, jnp.exp(scores - top), 0.0)
        probs = raised * (1.0 / jnp.sum(raised, axis=1, keepdims=True))
        pb = probs.astype(BF16)
        out = jnp.dot(pb, vv, preferred_element_type=F32)
        out = jnp.where(live, out, 0.0).astype(BF16)
        cols_o = pl.ds(pl.multiple_of(c * HALF + n * HEAD_DIM, HEAD_DIM), HEAD_DIM)

        @pl.when(h == c)
        def _():
            attn_o[:, cols_o] = out

        @pl.when(h != c)
        def _():
            attn[:, cols] = out

        dv = lax.dot_general(pb, gg, tn, preferred_element_type=F32).astype(BF16)
        dp = lax.dot_general(gg, vv, nt, preferred_element_type=F32)
        mid = jnp.sum(probs * dp, axis=1, keepdims=True)
        dsc = (probs * (dp - mid) * factor).astype(BF16)
        dq = jnp.dot(dsc, kk, preferred_element_type=F32).astype(BF16)
        dk = lax.dot_general(dsc, qq, tn, preferred_element_type=F32).astype(BF16)
        grads[rows, q_at] = dq
        grads[rows, k_at] = dk
        grads[rows, v_at] = dv
        terms = (
            dq.astype(F32) * qq.astype(F32)
            + dk.astype(F32) * kk.astype(F32)
            + dv.astype(F32) * vv.astype(F32)
        )
        stat[rows, :] += jnp.broadcast_to(jnp.sum(terms, axis=1, keepdims=True), (ROWS, 128))
        return carry

    stat[...] = jnp.zeros_like(stat)
    lax.fori_loop(0, 4, attend, 0, unroll=2)
    third(1, 2)
    def early(k, carry):
        dx0[k] = lax.dot_general(
            grads[:, 0:TRIO], wv[ds(k, UNIT), 0:TRIO], nt, preferred_element_type=F32
        )
        return carry

    lax.fori_loop(0, D // UNIT, early, 0)
    third(1, 3)
    project_near()
    last(1, (0, 1, 2))
    project_far()
    last(1, (3,))
    project_last()
    lax.fori_loop(4, 8, attend, 0, unroll=4)

    rows_own, rows_mate = ds(c, ROWS), ds(1 - c, ROWS)
    low, high = pl.ds(0, ROWS // 2), pl.ds(ROWS // 2, ROWS // 2)
    order = (x2, x1, x3, x)

    def back(q, n):
        u = q * 4 + n
        at = pl.ds(pl.multiple_of(order[n] * WIDTH + q * UNIT, UNIT), UNIT)
        late = lax.dot_general(
            grads[:, TRIO:ALL3], wv[at, TRIO:ALL3], nt, preferred_element_type=F32
        )
        dxs[u] = (late + dx0[order[n] * PIECES + q]).astype(BF16)
        sends.append(rcopy(dxs.at[u, rows_mate], cbuf.at[u], c_s.at[u], c_r.at[u], fsdp=mate))

    def summed(u):
        arrived(cbuf.at[u], c_r.at[u])
        pbuf[u] = (dxs[u, rows_own, :].astype(F32) + cbuf[u].astype(F32)).astype(BF16)

    def ring(q, k, src, dst, to):
        sends.append(rcopy(src, dst, r_s.at[q * 6 + k], r_r.at[q * 6 + k], tensor=to))

    def far_out(q):
        summed(q * 4)
        ring(q, 0, pbuf.at[q * 4, low], rfwd.at[q, 0], x1)
        ring(q, 1, pbuf.at[q * 4, high], rfwd.at[q, 1], x3)

    def near_out(q):
        summed(q * 4 + 1)
        ring(q, 2, pbuf.at[q * 4 + 1, high], rdir.at[q, 0, high], x1)
        summed(q * 4 + 2)
        ring(q, 3, pbuf.at[q * 4 + 2, low], rdir.at[q, 1, low], x3)

    def add_out(q):
        for k, rows, to in ((0, low, x1), (1, high, x3)):
            u = q * 4 + 1 + k
            arrived(rfwd.at[q, k], r_r.at[q * 6 + k])
            pbuf[u, rows, :] = (pbuf[u, rows, :].astype(F32) + rfwd[q, k].astype(F32)).astype(BF16)
            ring(q, 4 + k, pbuf.at[u, rows], rdir.at[q, k, rows], to)

    def a_out(q):
        for k, rows in ((0, high), (1, low)):
            arrived(rdir.at[q, k, rows], r_r.at[q * 6 + 2 + k])
        for k, rows in ((0, low), (1, high)):
            arrived(rdir.at[q, k, rows], r_r.at[q * 6 + 4 + k])
        at = pl.ds(pl.multiple_of(x * WIDTH + q * UNIT, UNIT), UNIT)
        parts = pbuf[q * 4 + 3].astype(F32) + rdir[q, 0].astype(F32) + rdir[q, 1].astype(F32)
        grad = iv * (parts * ugain[:, at]) - xh[c, :, at].astype(F32) * coef
        og[q] = jnp.dot(tt[...], grad.astype(BF16), preferred_element_type=F32).astype(BF16)

        def send(d, carry):
            to = lax.rem(f + d, NF)
            here, there = og.at[q, ds(to, CAP)], inc.at[ds(f, CAP), pl.ds(q * UNIT, UNIT)]
            rcopy(here, there, b_s.at[q], b_r.at[q], fsdp=to)
            return carry

        lax.fori_loop(1, NF, send, 0)
        keep = pltpu.make_async_copy(
            og.at[q, ds(f, CAP)], inc.at[ds(f, CAP), pl.ds(q * UNIT, UNIT)], loc.at[10 + q]
        )
        keep.start()
        return keep

    def stat_out():
        arrived(sbuf, st_r.at[4])
        both = stat[rows_own, :] + sbuf[...]
        srow[x] = jnp.transpose(both)[0:8, :]
        for n, to in enumerate((x1, x3, x2)):
            sends.append(rcopy(srow.at[x], srow.at[x], st_s.at[n], st_r.at[x], tensor=to))

    def stat_in():
        for frm in (x1, x3, x2):
            arrived(srow.at[frm], st_r.at[frm])
        total = (srow[0] + srow[1] + srow[2] + srow[3])[0:1, :]
        full_rows = jnp.transpose(jnp.broadcast_to(total, (128, ROWS)))
        iv = inv_h[rows_own, 0:1]
        coef = iv * iv * full_rows[:, 0:1] / D
        return iv, coef

    for q, n in ((0, 0), (0, 1), (0, 2), (1, 0)):
        back(q, n)
    sends.append(rcopy(stat.at[rows_mate], sbuf, st_s.at[3], st_r.at[4], fsdp=mate))
    far_out(0)
    back(1, 1)
    near_out(0)
    back(1, 2)
    far_out(1)
    stat_out()
    back(2, 0)
    back(2, 1)
    add_out(0)
    near_out(1)
    back(2, 2)
    back(0, 3)
    far_out(2)
    back(3, 0)
    back(1, 3)
    add_out(1)
    near_out(2)
    back(3, 1)
    back(3, 2)
    far_out(3)
    summed(3)
    iv, coef = stat_in()
    keeps = [a_out(0)]
    back(2, 3)
    back(3, 3)
    add_out(2)
    near_out(3)
    sends.append(rcopy(attn, attn_o.at[:, ds(c, HALF)], at_s, at_r, fsdp=mate))
    summed(7)
    keeps.append(a_out(1))
    add_out(3)
    summed(11)
    keeps.append(a_out(2))
    summed(15)
    keeps.append(a_out(3))

    for q in range(PIECES):
        arrived(inc.at[pl.ds(0, PEERS * CAP), pl.ds(q * UNIT, UNIT)], b_r.at[q])
        arrived(og.at[q, pl.ds(0, PEERS * CAP)], b_s.at[q])
    arrived(idb.at[pl.ds(0, PEERS)], id_s)
    arrived(fnd.at[pl.ds(0, PEERS * CAP)], a_s)
    arrived(attn_o.at[:, ds(1 - c, HALF)], at_r)
    for copy in keeps:
        copy.wait()
    for copy in sends:
        copy.wait_send()


ANY = pl.BlockSpec(memory_space=pl.ANY)
VMEM = pl.BlockSpec(memory_space=pltpu.VMEM)
DMA = pltpu.SemaphoreType.DMA


def layer(item_hidden, item_gain, wqkv, ids, grad_out, user_gain):
    vm = pltpu.VMEM
    return pl.pallas_call(
        layer_kernel,
        out_shape=(
            jax.ShapeDtypeStruct((ROWS, WIDTH), BF16),
            jax.ShapeDtypeStruct((SLOTS, ROWS), BF16),
            jax.ShapeDtypeStruct((ROWS, WIDTH), BF16),
            jax.ShapeDtypeStruct((SLOTS, WIDTH), BF16),
        ),
        in_specs=[ANY, VMEM, ANY, ANY, ANY, VMEM],
        out_specs=(VMEM, VMEM, VMEM, ANY),
        scratch_shapes=[
            vm((ROWS * ITEM_LEN, WIDTH), BF16),
            vm((NF, 8, ROWS), jnp.int32),
            vm((NX, 128, 128), F32),
            vm((128, 128), F32),
            vm((SLOTS, ROWS), BF16),
            vm((SLOTS, WIDTH), BF16),
            vm((SLOTS, WIDTH), BF16),
            vm((ROWS, WIDTH), BF16),
            vm((D, ALL3), BF16),
            vm((2, ROWS, D), BF16),
            vm((BOTH, D), BF16),
            vm((BOTH, TRIO), F32),
            vm((BOTH, ALL3), BF16),
            vm((BOTH, ALL3), BF16),
            vm((2, ROWS, HALF), BF16),
            vm((ROWS, HALF), BF16),
            vm((BOTH, 128), F32),
            vm((BOTH, 128), F32),
            vm((ROWS, 128), F32),
            vm((NX, 8, ROWS), F32),
            vm((4 * PIECES, BOTH, UNIT), F32),
            vm((4 * PIECES, BOTH, UNIT), BF16),
            vm((4 * PIECES, ROWS, UNIT), BF16),
            vm((4 * PIECES, ROWS, UNIT), BF16),
            vm((PIECES, 2, ROWS, UNIT), BF16),
            vm((PIECES, 2, ROWS // 2, UNIT), BF16),
            vm((PIECES, SLOTS, UNIT), BF16),
            DMA((10 + PIECES,)),
            DMA, DMA,
            DMA((3,)), DMA((NX,)),
            DMA, DMA,
            DMA((80,)), DMA((4 * NF,)),
            DMA((6,)), DMA((6,)),
            DMA((6,)), DMA((2 * NX,)),
            DMA((4,)), DMA((NX,)),
            DMA, DMA,
            DMA, DMA,
            DMA((4,)), DMA((5,)),
            DMA((4 * PIECES,)), DMA((4 * PIECES,)),
            DMA((6 * PIECES,)), DMA((6 * PIECES,)),
            DMA((PIECES,)), DMA((PIECES,)),
        ],
        compiler_params=pltpu.CompilerParams(
            collective_id=0, has_side_effects=True, vmem_limit_bytes=62 * MIB
        ),
        cost_estimate=pl.CostEstimate(flops=27 * 10**9, bytes_accessed=64 * MIB, transcendentals=10**6),
        name="layer",
    )(item_hidden, item_gain, wqkv, ids, grad_out, user_gain)


def closing_kernel(emb, attn, oh, inc, emb_o, attn_o, grads_o, oh_v, inc_v, emb_v, attn_v, sem):
    pairs = ((oh, oh_v), (inc, inc_v), (emb, emb_v), (attn, attn_v), (emb_v, emb_o), (attn_v, attn_o))
    copies = [pltpu.make_async_copy(src, dst, sem.at[n]) for n, (src, dst) in enumerate(pairs)]
    for copy in copies[:4]:
        copy.start()
    for n in (2, 3):
        copies[n].wait()
        copies[n + 2].start()
    for copy in copies[:2]:
        copy.wait()
    grads_o[...] = lax.dot_general(
        oh_v[...], inc_v[...], (((0,), (0,)), ((), ())), preferred_element_type=F32
    )
    for copy in copies[4:]:
        copy.wait()


def closing(item_embed, attended, wanted, incoming):
    return pl.pallas_call(
        closing_kernel,
        out_shape=(
            jax.ShapeDtypeStruct((ROWS, WIDTH), BF16),
            jax.ShapeDtypeStruct((ROWS, WIDTH), BF16),
            jax.ShapeDtypeStruct((ROWS, WIDTH), F32),
        ),
        in_specs=[ANY] * 4,
        out_specs=(ANY, ANY, VMEM),
        scratch_shapes=[
            pltpu.VMEM((SLOTS, ROWS), BF16),
            pltpu.VMEM((SLOTS, WIDTH), BF16),
            pltpu.VMEM((ROWS, WIDTH), BF16),
            pltpu.VMEM((ROWS, WIDTH), BF16),
            DMA((6,)),
        ],
        compiler_params=pltpu.CompilerParams(vmem_limit_bytes=62 * MIB),
        cost_estimate=pl.CostEstimate(flops=3 * 10**8, bytes_accessed=5 * MIB, transcendentals=0),
        name="closing",
    )(item_embed, attended, wanted, incoming)


def on_device(item_hidden, item_gain, occ_owner, occ_item, hist_len, user_gain, wqkv, grad_out):
    ids = jnp.stack(
        [occ_owner[:, 0], occ_item, jnp.broadcast_to(hist_len, (ROWS,))]
        + [jnp.zeros((ROWS,), jnp.int32)] * 5
    )
    item_embed, wanted, attended, incoming = layer(
        item_hidden, item_gain.reshape(1, WIDTH), wqkv, ids, grad_out, user_gain.reshape(1, D)
    )
    return closing(item_embed, attended, wanted, incoming)


def solution(mesh):
    in_specs = (
        P("fsdp", "tensor"),
        P("tensor"),
        P("fsdp", None),
        P("fsdp"),
        P("fsdp"),
        P(),
        P(None, "fsdp", "tensor"),
        P("fsdp", "tensor"),
    )
    out_specs = (P("fsdp", "tensor"), P("fsdp", "tensor"), P("fsdp", "tensor"))
    return jax.shard_map(
        on_device, mesh=mesh, in_specs=in_specs, out_specs=out_specs, check_vma=False
    )
```

```python
import functools
import math

import jax
import jax.numpy as jnp
from jax import lax
from jax.experimental import pallas as pl
from jax.experimental.pallas import tpu as pltpu
from jax.sharding import PartitionSpec as P

D = 4096
HEAD_DIM = 128
ITEM_LEN = 8
EPSILON = 1e-05
NF = 32
NX = 4
ROWS = 256
CAP = 16
SLOTS = NF * CAP
WIDTH = D // NX
HALF = WIDTH // 2
SHARD = D // NF
GROUP = HALF // 2
TRIO = 3 * GROUP
PIECES = 4
UNIT = WIDTH // PIECES
PEERS = NF - 1
ALL3 = 2 * TRIO
BOTH = 2 * ROWS
F32 = jnp.float32
BF16 = jnp.bfloat16
MIB = 1 << 20


def rcopy(src, dst, send, recv, **where):
    copy = pltpu.make_async_remote_copy(
        src_ref=src,
        dst_ref=dst,
        send_sem=send,
        recv_sem=recv,
        device_id=where,
        device_id_type=pl.DeviceIdType.MESH,
    )
    copy.start()
    return copy


def arrived(ref, sem):
    pltpu.make_async_copy(ref, ref, sem).wait()


def greet():
    f, x = lax.axis_index("fsdp"), lax.axis_index("tensor")
    barrier = pltpu.get_barrier_semaphore()

    def signal(d, carry):
        pl.semaphore_signal(
            barrier,
            inc=1,
            device_id={"fsdp": lax.rem(f + d, NF)},
            device_id_type=pl.DeviceIdType.MESH,
        )
        return carry

    lax.fori_loop(1, NF, signal, 0)
    for d in range(1, NX):
        pl.semaphore_signal(
            barrier,
            inc=1,
            device_id={"tensor": lax.rem(x + d, NX)},
            device_id_type=pl.DeviceIdType.MESH,
        )


def greeted():
    pl.semaphore_wait(pltpu.get_barrier_semaphore(), NF - 1 + NX - 1)


def layer_kernel(
    hid, gain, w, ids, g, ugain,
    emb_o, oh_o, attn_o, inc,
    hid_v, idb, sqb, inv_v, tt, fnd, fet, share,
    wv, xh, nrm, acc, qkv, grads, gv, attn, inv_h, stat, sbuf, srow,
    dx0, dxs, cbuf, pbuf, rdir, rfwd, og,
    loc, id_s, id_r, sq_s, sq_r, a_s, a_r, w_s, w_r, wm_s, wm_r,
    x_s, x_r, p_s, p_r, g_s, g_r, at_s, at_r, st_s, st_r,
    c_s, c_r, r_s, r_r, b_s, b_r,
):
    f, x = lax.axis_index("fsdp"), lax.axis_index("tensor")
    c = lax.rem(f, 2)
    chip = f // 2
    z, y = lax.rem(chip, 4), chip // 4
    mate = f + 1 - 2 * c
    y1, y2, y3 = (lax.rem(y + d, 4) for d in (1, 2, 3))
    z1, z2, z3 = (lax.rem(z + d, 4) for d in (1, 2, 3))
    x1, x2, x3 = (lax.rem(x + d, 4) for d in (1, 2, 3))
    at_chip = lambda yy, zz: yy * 4 + zz
    yp, ym = at_chip(y1, z) * 2 + c, at_chip(y3, z) * 2 + c
    zp, zm = at_chip(y, z1) * 2 + c, at_chip(y, z3) * 2 + c
    sends = []

    def ds(i, n):
        return pl.ds(pl.multiple_of(i * n, n), n)

    load_hid = pltpu.make_async_copy(hid, hid_v, loc.at[0])
    load_hid.start()
    keep_w = []
    for h in range(2):
        for n in range(3):
            src = w.at[n, :, pl.ds(pl.multiple_of(c * HALF + h * GROUP, GROUP), GROUP)]
            dst = wv.at[ds(f, SHARD), pl.ds(h * TRIO + n * GROUP, GROUP)]
            keep_w.append(pltpu.make_async_copy(src, dst, loc.at[4 + h * 3 + n]))
            keep_w[-1].start()
    keep_id = pltpu.make_async_copy(ids, idb.at[f], loc.at[1])
    keep_id.start()
    keep_g = pltpu.make_async_copy(g.at[:, ds(c, HALF)], gv.at[c], loc.at[2])
    keep_g.start()
    greet()

    lane = lax.broadcasted_iota(jnp.int32, (128, 128), 1)

    def squares(k, total):
        v = hid_v[ds(k, 128), :].astype(F32)
        return jnp.where(lane == k, jnp.sum(v * v, axis=1, keepdims=True), total)

    greeted()

    def piece(h, s):
        return wv.at[ds(s, SHARD), pl.ds(h * TRIO, TRIO)]

    def part(h, s, k):
        at = pl.multiple_of(s * SHARD + k * (SHARD // 2), SHARD // 2)
        return wv.at[pl.ds(at, SHARD // 2), pl.ds(h * TRIO, TRIO)]

    wcount = [0]

    def wsend(ref, sem, dev):
        sends.append(rcopy(ref, ref, w_s.at[wcount[0]], w_r.at[sem], fsdp=dev))
        wcount[0] += 1

    def full(h, s, devs):
        for dev in devs:
            wsend(piece(h, s), (h * NF + s) * 2, dev)

    def half(h, s, k, dev):
        wsend(part(h, s, k), (h * NF + s) * 2 + k, dev)

    def got(h, s):
        arrived(piece(h, s), w_r.at[(h * NF + s) * 2])

    def got_halves(h, s):
        for k in range(2):
            arrived(part(h, s, k), w_r.at[(h * NF + s) * 2 + k])

    ways = ((yp, ym), (zp, zm))
    prev = (at_chip(y3, z) * 2, at_chip(y, z3) * 2 + 1)
    nxt = (at_chip(y1, z) * 2, at_chip(y, z1) * 2 + 1)
    far = (at_chip(y2, z) * 2, at_chip(y, z2) * 2 + 1)
    own = (chip * 2, chip * 2 + 1)

    for h in range(2):
        for n in range(3):
            src = w.at[n, :, pl.ds(pl.multiple_of((1 - c) * HALF + h * GROUP, GROUP), GROUP)]
            dst = wv.at[ds(f, SHARD), pl.ds(h * TRIO + n * GROUP, GROUP)]
            sends.append(rcopy(src, dst, wm_s.at[h * 3 + n], wm_r.at[h * 3 + n], fsdp=mate))
    first = (lax.select(c == 0, yp, zp), lax.select(c == 0, ym, zm))
    second = (lax.select(c == 0, zp, yp), lax.select(c == 0, zm, ym))
    for h in range(2):
        for copy in keep_w[3 * h : 3 * h + 3]:
            copy.wait()
        full(h, f, first)
        full(h, f, second)
    load_hid.wait()
    sqb[x] = lax.fori_loop(0, 16, squares, jnp.zeros((128, 128), F32))
    for n, to in enumerate((x1, x3, x2)):
        sends.append(rcopy(sqb.at[x], sqb.at[x], sq_s.at[n], sq_r.at[x], tensor=to))

    def id_send(d, carry):
        rcopy(ids, idb.at[f], id_s, id_r, fsdp=lax.rem(f + d, NF))
        return carry

    lax.fori_loop(1, NF, id_send, 0)
    sends.append(rcopy(g.at[:, ds(1 - c, HALF)], gv.at[c], g_s, g_r, fsdp=mate))

    for h in range(2):
        for n in range(3):
            dst = wv.at[ds(mate, SHARD), pl.ds(h * TRIO + n * GROUP, GROUP)]
            arrived(dst, wm_r.at[h * 3 + n])
        full(h, mate, second)
        full(h, mate, first)

    def second_near(h):
        for r in range(2):
            got(h, prev[r])
            half(h, prev[r], 0, ways[r][0])
            got(h, nxt[r])
            half(h, nxt[r], 1, ways[r][1])
        for r in range(2):
            full(h, prev[r], ways[1 - r])
            full(h, nxt[r], ways[1 - r])

    def second_far(h):
        for r in range(2):
            got_halves(h, far[r])
            full(h, far[r], ways[1 - r])

    def third(h, n):
        yy, zz = ((y, z), (y3, z3), (y1, z1), (y2, z2))[n]
        low = (at_chip(yy, z3) * 2, at_chip(y3, zz) * 2 + 1)
        high = (at_chip(yy, z1) * 2, at_chip(y1, zz) * 2 + 1)
        for r in range(2):
            got(h, low[r])
            half(h, low[r], 0, ways[1 - r][0])
            got(h, high[r])
            half(h, high[r], 1, ways[1 - r][1])

    def last(h, which):
        for n in which:
            yy, zz = ((y, z), (y3, z3), (y1, z1), (y2, z2))[n]
            got_halves(h, at_chip(yy, z2) * 2)
            got_halves(h, at_chip(y2, zz) * 2 + 1)

    arrived(idb.at[pl.ds(0, PEERS)], id_r)
    keep_id.wait()
    row = lax.broadcasted_iota(jnp.int32, (SLOTS, ROWS), 0)
    col = lax.broadcasted_iota(jnp.int32, (SLOTS, ROWS), 1)
    slot = lax.rem(row, CAP).astype(F32)
    group = row // CAP
    t_at = lax.broadcasted_iota(jnp.int32, (ROWS, ROWS), 0)
    s_at = lax.broadcasted_iota(jnp.int32, (ROWS, ROWS), 1)
    before = (t_at < s_at).astype(F32).astype(BF16)

    def slots_of(named):
        rank = jnp.dot(named.astype(F32).astype(BF16), before, preferred_element_type=F32)
        return named & (rank == slot)

    mine_owner = jnp.broadcast_to(idb[f, 0:1, :], (SLOTS, ROWS))
    tt[...] = slots_of(mine_owner == group).astype(F32).astype(BF16)
    table = idb[...].reshape(NF * 8, ROWS).astype(F32).astype(BF16)
    pick_owner = (col == group * 8).astype(F32).astype(BF16)
    pick_item = (col == group * 8 + 1).astype(F32).astype(BF16)
    owner_all = jnp.dot(pick_owner, table, preferred_element_type=F32)
    item_all = jnp.dot(pick_item, table, preferred_element_type=F32)
    taken = slots_of(owner_all == f.astype(F32))
    wanted = jnp.sum(jnp.where(taken, item_all + 1.0, 0.0), axis=1, keepdims=True) - 1.0
    oh_o[...] = (wanted == col.astype(F32)).astype(F32).astype(BF16)

    for frm in (x1, x3, x2):
        arrived(sqb.at[frm], sq_r.at[frm])
    inv_v[...] = lax.rsqrt((sqb[0] + sqb[1] + sqb[2] + sqb[3]) / D + EPSILON)

    def pool(k, carry):
        v = hid_v[ds(k, 128), :].astype(F32)
        inv = jnp.sum(jnp.where(lane == k, inv_v[...], 0.0), axis=1, keepdims=True)
        total = jnp.sum((v * inv).reshape(16, ITEM_LEN, WIDTH), axis=1)
        emb_o[ds(k, 16), :] = (total * (1.0 / ITEM_LEN) * gain[...]).astype(BF16)
        return carry

    lax.fori_loop(0, 16, pool, 0)
    fnd[...] = jnp.dot(oh_o[...], emb_o[...], preferred_element_type=F32).astype(BF16)

    def a_send(d, carry):
        to = lax.rem(f + d, NF)
        rcopy(fnd.at[ds(to, CAP)], fet.at[ds(f, CAP)], a_s, a_r, fsdp=to)
        return carry

    lax.fori_loop(1, NF, a_send, 0)
    fet[ds(f, CAP), :] = fnd[ds(f, CAP), :]
    second_near(0)
    third(0, 0)

    arrived(fet.at[pl.ds(0, PEERS * CAP)], a_r)
    share[...] = lax.dot_general(
        tt[...], fet[...], (((0,), (0,)), ((), ())), preferred_element_type=F32
    ).astype(BF16)

    def xpart(j, h):
        return xh.at[c, pl.ds(h * (ROWS // 2), ROWS // 2), ds(j, WIDTH)]

    def xwhole(k, j):
        return xh.at[k, :, ds(j, WIDTH)]

    keep_x = pltpu.make_async_copy(share, xwhole(c, x), loc.at[3])
    keep_x.start()
    for h in range(2):
        rows = share.at[pl.ds(h * (ROWS // 2), ROWS // 2)]
        sends.append(rcopy(rows, xpart(x, h), x_s.at[h], x_r.at[2 * x + h], tensor=x1))
        sends.append(rcopy(rows, xpart(x, h), x_s.at[2 + h], x_r.at[2 * x + h], tensor=x3))
    sends.append(rcopy(share, xwhole(c, x), p_s.at[0], p_r.at[x], fsdp=mate))

    def x_forward():
        for h, (frm, to) in enumerate(((x3, x1), (x1, x3))):
            arrived(xpart(frm, h), x_r.at[2 * frm + h])
            sends.append(rcopy(xpart(frm, h), xpart(frm, h), x_s.at[4 + h], x_r.at[2 * frm + h], tensor=to))
        for h, frm in enumerate((x3, x1)):
            arrived(xpart(frm, 1 - h), x_r.at[2 * frm + 1 - h])
            sends.append(rcopy(xwhole(c, frm), xwhole(c, frm), p_s.at[1 + h], p_r.at[frm], fsdp=mate))

    def x_finish():
        for h in range(2):
            arrived(xpart(x2, h), x_r.at[2 * x2 + h])
        sends.append(rcopy(xwhole(c, x2), xwhole(c, x2), p_s.at[3], p_r.at[x2], fsdp=mate))
        keep_x.wait()

    def norm(k, carry):
        h, m = k // 8, lax.rem(k, 8)
        v = xh[h, ds(m, 32), :].astype(F32)
        inv = lax.rsqrt(jnp.sum(v * v, axis=1, keepdims=True) / D + EPSILON)
        nrm[ds(k, 32), :] = (v * inv * ugain[...]).astype(BF16)
        inv_h[ds(k, 32), :] = jnp.broadcast_to(inv, (32, 128))
        return carry

    def project(k):
        acc[...] += jnp.dot(
            nrm[:, ds(k, 256)], wv[ds(k, 256), TRIO:ALL3], preferred_element_type=F32
        )

    def project_near():
        def block(t, carry):
            yy, zz = lax.rem(y + 3 + t // 3, 4), lax.rem(z + 3 + lax.rem(t, 3), 4)
            project(at_chip(yy, zz))
            return carry

        lax.fori_loop(0, 9, block, 0, unroll=3)

    def project_far():
        def block(t, carry):
            yy, zz = lax.rem(y + 3 + t, 4), lax.rem(z + 3 + t, 4)
            project(at_chip(yy, z2))
            project(at_chip(y2, zz))
            return carry

        lax.fori_loop(0, 3, block, 0)

    def project_last():
        project(at_chip(y2, z2))
        qkv[:, TRIO:ALL3] = acc[...].astype(BF16)

    acc[...] = jnp.zeros_like(acc)
    second_far(0)
    third(0, 1)
    third(0, 2)
    x_forward()
    third(0, 3)
    second_near(1)
    third(1, 0)
    x_finish()
    lax.fori_loop(c * 8, c * 8 + 8, norm, 0)
    second_far(1)
    for j in (x, x3, x1, x2):
        arrived(xwhole(1 - c, j), p_r.at[j])
    lax.fori_loop((1 - c) * 8, (1 - c) * 8 + 8, norm, 0)
    last(0, (0, 1, 2, 3))

    def project_all(n, carry):
        at = ds(n, GROUP)
        qkv[:, at] = jnp.dot(nrm[...], wv[:, at], preferred_element_type=F32).astype(BF16)
        return carry

    lax.fori_loop(0, 3, project_all, 0)
    third(1, 1)

    factor = 1.0 / math.sqrt(HEAD_DIM)
    t_row = lax.broadcasted_iota(jnp.int32, (ROWS, HEAD_DIM), 0)
    nt = (((1,), (1,)), ((), ()))
    tn = (((0,), (0,)), ((), ()))
    keep_g.wait()
    arrived(gv.at[1 - c], g_r)

    def attend(k, carry):
        h, n = lax.rem(k, 2), k // 2
        rows = ds(h, ROWS)
        cols = ds(n, HEAD_DIM)
        base = (n // 2) * TRIO + lax.rem(n, 2) * HEAD_DIM
        q_at, k_at, v_at = (
            pl.ds(pl.multiple_of(base + i * GROUP, HEAD_DIM), HEAD_DIM) for i in range(3)
        )
        length = idb[chip * 2 + h, 2:3, :]
        allowed = (s_at <= t_at) & (s_at < length)
        live = t_row < length[:, :HEAD_DIM]
        qq, kk, vv = qkv[rows, q_at], qkv[rows, k_at], qkv[rows, v_at]
        gg = jnp.where(live, gv[h, :, cols].astype(F32), 0.0).astype(BF16)
        scores = lax.dot_general(qq, kk, nt, preferred_element_type=F32) * factor
        scores = jnp.where(allowed, scores, -1e30)
        top = jnp.max(scores, axis=1, keepdims=True)
        raised = jnp.where(allowed, jnp.exp(scores - top), 0.0)
        probs = raised * (1.0 / jnp.sum(raised, axis=1, keepdims=True))
        pb = probs.astype(BF16)
        out = jnp.dot(pb, vv, preferred_element_type=F32)
        out = jnp.where(live, out, 0.0).astype(BF16)
        cols_o = pl.ds(pl.multiple_of(c * HALF + n * HEAD_DIM, HEAD_DIM), HEAD_DIM)

        @pl.when(h == c)
        def _():
            attn_o[:, cols_o] = out

        @pl.when(h != c)
        def _():
            attn[:, cols] = out

        dv = lax.dot_general(pb, gg, tn, preferred_element_type=F32).astype(BF16)
        dp = lax.dot_general(gg, vv, nt, preferred_element_type=F32)
        mid = jnp.sum(probs * dp, axis=1, keepdims=True)
        dsc = (probs * (dp - mid) * factor).astype(BF16)
        dq = jnp.dot(dsc, kk, preferred_element_type=F32).astype(BF16)
        dk = lax.dot_general(dsc, qq, tn, preferred_element_type=F32).astype(BF16)
        grads[rows, q_at] = dq
        grads[rows, k_at] = dk
        grads[rows, v_at] = dv
        terms = (
            dq.astype(F32) * qq.astype(F32)
            + dk.astype(F32) * kk.astype(F32)
            + dv.astype(F32) * vv.astype(F32)
        )
        stat[rows, :] += jnp.broadcast_to(jnp.sum(terms, axis=1, keepdims=True), (ROWS, 128))
        return carry

    stat[...] = jnp.zeros_like(stat)
    lax.fori_loop(0, 4, attend, 0, unroll=2)
    third(1, 2)
    def early(k, carry):
        dx0[k] = lax.dot_general(
            grads[:, 0:TRIO], wv[ds(k, UNIT), 0:TRIO], nt, preferred_element_type=F32
        )
        return carry

    lax.fori_loop(0, D // UNIT, early, 0, unroll=4)
    third(1, 3)
    project_near()
    last(1, (0, 1, 2))
    project_far()
    last(1, (3,))
    project_last()
    lax.fori_loop(4, 8, attend, 0, unroll=4)

    rows_own, rows_mate = ds(c, ROWS), ds(1 - c, ROWS)
    low, high = pl.ds(0, ROWS // 2), pl.ds(ROWS // 2, ROWS // 2)
    order = (x2, x1, x3, x)

    def back(q, n):
        u = q * 4 + n
        at = pl.ds(pl.multiple_of(order[n] * WIDTH + q * UNIT, UNIT), UNIT)
        late = lax.dot_general(
            grads[:, TRIO:ALL3], wv[at, TRIO:ALL3], nt, preferred_element_type=F32
        )
        dxs[u] = (late + dx0[order[n] * PIECES + q]).astype(BF16)
        sends.append(rcopy(dxs.at[u, rows_mate], cbuf.at[u], c_s.at[u], c_r.at[u], fsdp=mate))

    def summed(u):
        arrived(cbuf.at[u], c_r.at[u])
        pbuf[u] = (dxs[u, rows_own, :].astype(F32) + cbuf[u].astype(F32)).astype(BF16)

    def ring(q, k, src, dst, to):
        sends.append(rcopy(src, dst, r_s.at[q * 6 + k], r_r.at[q * 6 + k], tensor=to))

    def far_out(q):
        summed(q * 4)
        ring(q, 0, pbuf.at[q * 4, low], rfwd.at[q, 0], x1)
        ring(q, 1, pbuf.at[q * 4, high], rfwd.at[q, 1], x3)

    def near_out(q):
        summed(q * 4 + 1)
        ring(q, 2, pbuf.at[q * 4 + 1, high], rdir.at[q, 0, high], x1)
        summed(q * 4 + 2)
        ring(q, 3, pbuf.at[q * 4 + 2, low], rdir.at[q, 1, low], x3)

    def add_out(q):
        for k, rows, to in ((0, low, x1), (1, high, x3)):
            u = q * 4 + 1 + k
            arrived(rfwd.at[q, k], r_r.at[q * 6 + k])
            pbuf[u, rows, :] = (pbuf[u, rows, :].astype(F32) + rfwd[q, k].astype(F32)).astype(BF16)
            ring(q, 4 + k, pbuf.at[u, rows], rdir.at[q, k, rows], to)

    def a_out(q):
        for k, rows in ((0, high), (1, low)):
            arrived(rdir.at[q, k, rows], r_r.at[q * 6 + 2 + k])
        for k, rows in ((0, low), (1, high)):
            arrived(rdir.at[q, k, rows], r_r.at[q * 6 + 4 + k])
        at = pl.ds(pl.multiple_of(x * WIDTH + q * UNIT, UNIT), UNIT)
        parts = pbuf[q * 4 + 3].astype(F32) + rdir[q, 0].astype(F32) + rdir[q, 1].astype(F32)
        grad = iv * (parts * ugain[:, at]) - xh[c, :, at].astype(F32) * coef
        og[q] = jnp.dot(tt[...], grad.astype(BF16), preferred_element_type=F32).astype(BF16)

        def send(d, carry):
            to = lax.rem(f + d, NF)
            here, there = og.at[q, ds(to, CAP)], inc.at[ds(f, CAP), pl.ds(q * UNIT, UNIT)]
            rcopy(here, there, b_s.at[q], b_r.at[q], fsdp=to)
            return carry

        lax.fori_loop(1, NF, send, 0)
        keep = pltpu.make_async_copy(
            og.at[q, ds(f, CAP)], inc.at[ds(f, CAP), pl.ds(q * UNIT, UNIT)], loc.at[10 + q]
        )
        keep.start()
        return keep

    def stat_out():
        arrived(sbuf, st_r.at[4])
        both = stat[rows_own, :] + sbuf[...]
        srow[x] = jnp.transpose(both)[0:8, :]
        for n, to in enumerate((x1, x3, x2)):
            sends.append(rcopy(srow.at[x], srow.at[x], st_s.at[n], st_r.at[x], tensor=to))

    def stat_in():
        for frm in (x1, x3, x2):
            arrived(srow.at[frm], st_r.at[frm])
        total = (srow[0] + srow[1] + srow[2] + srow[3])[0:1, :]
        full_rows = jnp.transpose(jnp.broadcast_to(total, (128, ROWS)))
        iv = inv_h[rows_own, 0:1]
        coef = iv * iv * full_rows[:, 0:1] / D
        return iv, coef

    back(0, 0)
    back(0, 1)
    back(0, 2)
    sends.append(rcopy(stat.at[rows_mate], sbuf, st_s.at[3], st_r.at[4], fsdp=mate))
    back(1, 0)
    far_out(0)
    back(1, 1)
    near_out(0)
    back(1, 2)
    far_out(1)
    stat_out()
    back(2, 0)
    back(2, 1)
    back(2, 2)
    add_out(0)
    near_out(1)
    far_out(2)
    back(0, 3)
    back(3, 0)
    summed(3)
    back(3, 1)
    back(3, 2)
    add_out(1)
    near_out(2)
    iv, coef = stat_in()
    keeps = []
    far_out(3)
    keeps.append(a_out(0))
    back(1, 3)
    back(2, 3)
    summed(7)
    add_out(2)
    near_out(3)
    keeps.append(a_out(1))
    back(3, 3)
    summed(11)
    add_out(3)
    keeps.append(a_out(2))
    summed(15)
    keeps.append(a_out(3))
    sends.append(rcopy(attn, attn_o.at[:, ds(c, HALF)], at_s, at_r, fsdp=mate))

    for q in range(PIECES):
        arrived(inc.at[pl.ds(0, PEERS * CAP), pl.ds(q * UNIT, UNIT)], b_r.at[q])
        arrived(og.at[q, pl.ds(0, PEERS * CAP)], b_s.at[q])
    arrived(idb.at[pl.ds(0, PEERS)], id_s)
    arrived(fnd.at[pl.ds(0, PEERS * CAP)], a_s)
    arrived(attn_o.at[:, ds(1 - c, HALF)], at_r)
    for copy in keeps:
        copy.wait()
    for copy in sends:
        copy.wait_send()


ANY = pl.BlockSpec(memory_space=pl.ANY)
VMEM = pl.BlockSpec(memory_space=pltpu.VMEM)
DMA = pltpu.SemaphoreType.DMA


def layer(item_hidden, item_gain, wqkv, ids, grad_out, user_gain):
    vm = pltpu.VMEM
    return pl.pallas_call(
        layer_kernel,
        out_shape=(
            jax.ShapeDtypeStruct((ROWS, WIDTH), BF16),
            jax.ShapeDtypeStruct((SLOTS, ROWS), BF16),
            jax.ShapeDtypeStruct((ROWS, WIDTH), BF16),
            jax.ShapeDtypeStruct((SLOTS, WIDTH), BF16),
        ),
        in_specs=[ANY, VMEM, ANY, ANY, ANY, VMEM],
        out_specs=(VMEM, VMEM, VMEM, ANY),
        scratch_shapes=[
            vm((ROWS * ITEM_LEN, WIDTH), BF16),
            vm((NF, 8, ROWS), jnp.int32),
            vm((NX, 128, 128), F32),
            vm((128, 128), F32),
            vm((SLOTS, ROWS), BF16),
            vm((SLOTS, WIDTH), BF16),
            vm((SLOTS, WIDTH), BF16),
            vm((ROWS, WIDTH), BF16),
            vm((D, ALL3), BF16),
            vm((2, ROWS, D), BF16),
            vm((BOTH, D), BF16),
            vm((BOTH, TRIO), F32),
            vm((BOTH, ALL3), BF16),
            vm((BOTH, ALL3), BF16),
            vm((2, ROWS, HALF), BF16),
            vm((ROWS, HALF), BF16),
            vm((BOTH, 128), F32),
            vm((BOTH, 128), F32),
            vm((ROWS, 128), F32),
            vm((NX, 8, ROWS), F32),
            vm((4 * PIECES, BOTH, UNIT), F32),
            vm((4 * PIECES, BOTH, UNIT), BF16),
            vm((4 * PIECES, ROWS, UNIT), BF16),
            vm((4 * PIECES, ROWS, UNIT), BF16),
            vm((PIECES, 2, ROWS, UNIT), BF16),
            vm((PIECES, 2, ROWS // 2, UNIT), BF16),
            vm((PIECES, SLOTS, UNIT), BF16),
            DMA((10 + PIECES,)),
            DMA, DMA,
            DMA((3,)), DMA((NX,)),
            DMA, DMA,
            DMA((80,)), DMA((4 * NF,)),
            DMA((6,)), DMA((6,)),
            DMA((6,)), DMA((2 * NX,)),
            DMA((4,)), DMA((NX,)),
            DMA, DMA,
            DMA, DMA,
            DMA((4,)), DMA((5,)),
            DMA((4 * PIECES,)), DMA((4 * PIECES,)),
            DMA((6 * PIECES,)), DMA((6 * PIECES,)),
            DMA((PIECES,)), DMA((PIECES,)),
        ],
        compiler_params=pltpu.CompilerParams(
            collective_id=0, has_side_effects=True, vmem_limit_bytes=62 * MIB
        ),
        cost_estimate=pl.CostEstimate(flops=27 * 10**9, bytes_accessed=64 * MIB, transcendentals=10**6),
        name="layer",
    )(item_hidden, item_gain, wqkv, ids, grad_out, user_gain)


def closing_kernel(emb, attn, oh, inc, emb_o, attn_o, grads_o, oh_v, inc_v, emb_v, attn_v, sem):
    pairs = ((oh, oh_v), (inc, inc_v), (emb, emb_v), (attn, attn_v), (emb_v, emb_o), (attn_v, attn_o))
    copies = [pltpu.make_async_copy(src, dst, sem.at[n]) for n, (src, dst) in enumerate(pairs)]
    for copy in copies[:4]:
        copy.start()
    for n in (2, 3):
        copies[n].wait()
        copies[n + 2].start()
    for copy in copies[:2]:
        copy.wait()
    grads_o[...] = lax.dot_general(
        oh_v[...], inc_v[...], (((0,), (0,)), ((), ())), preferred_element_type=F32
    )
    for copy in copies[4:]:
        copy.wait()


def closing(item_embed, attended, wanted, incoming):
    return pl.pallas_call(
        closing_kernel,
        out_shape=(
            jax.ShapeDtypeStruct((ROWS, WIDTH), BF16),
            jax.ShapeDtypeStruct((ROWS, WIDTH), BF16),
            jax.ShapeDtypeStruct((ROWS, WIDTH), F32),
        ),
        in_specs=[ANY] * 4,
        out_specs=(ANY, ANY, VMEM),
        scratch_shapes=[
            pltpu.VMEM((SLOTS, ROWS), BF16),
            pltpu.VMEM((SLOTS, WIDTH), BF16),
            pltpu.VMEM((ROWS, WIDTH), BF16),
            pltpu.VMEM((ROWS, WIDTH), BF16),
            DMA((6,)),
        ],
        compiler_params=pltpu.CompilerParams(vmem_limit_bytes=62 * MIB),
        cost_estimate=pl.CostEstimate(flops=3 * 10**8, bytes_accessed=5 * MIB, transcendentals=0),
        name="closing",
    )(item_embed, attended, wanted, incoming)


def on_device(item_hidden, item_gain, occ_owner, occ_item, hist_len, user_gain, wqkv, grad_out):
    ids = jnp.stack(
        [occ_owner[:, 0], occ_item, jnp.broadcast_to(hist_len, (ROWS,))]
        + [jnp.zeros((ROWS,), jnp.int32)] * 5
    )
    item_embed, wanted, attended, incoming = layer(
        item_hidden, item_gain.reshape(1, WIDTH), wqkv, ids, grad_out, user_gain.reshape(1, D)
    )
    return closing(item_embed, attended, wanted, incoming)


def solution(mesh):
    in_specs = (
        P("fsdp", "tensor"),
        P("tensor"),
        P("fsdp", None),
        P("fsdp"),
        P("fsdp"),
        P(),
        P(None, "fsdp", "tensor"),
        P("fsdp", "tensor"),
    )
    out_specs = (P("fsdp", "tensor"), P("fsdp", "tensor"), P("fsdp", "tensor"))
    return jax.shard_map(
        on_device, mesh=mesh, in_specs=in_specs, out_specs=out_specs, check_vma=False
    )
```
